128 devices in a mesh: space: 64 (over y, z, x), batch: 2 (over core).
Axes of the slice: x: 4, y: 4, z: 4, core: 2. Of those that a mesh axis runs over, the one named last changes fastest.
Arguments:
- volume: bfloat16 [4, 2, 256, 128, 128], P(None, 'batch', 'space'), may hold values from -72 to 72
- kernel_one: bfloat16 [108, 32], replicated, may hold values from -0.625 to 0.625
- kernel_two: bfloat16 [864, 64], replicated, may hold values from -0.21875 to 0.21875
- cotangent: bfloat16 [64, 2, 64, 1024], P(None, 'batch', 'space'), may hold values from -6 to 6
Outputs:
- features: bfloat16 [64, 2, 64, 1024], P(None, 'batch', None, 'space')
- factor_in_one: float32 [108, 108], replicated
- factor_in_two: float32 [864, 864], replicated
- factor_out_one: float32 [32, 32], replicated
- factor_out_two: float32 [64, 64], replicated
- weight_grad_one: float32 [108, 32], replicated
- weight_grad_two: float32 [864, 64], replicated
The draws below stay inside these ranges and needn't reach their ends.
All inputs are finite; a program needn't handle non-finite values.
Results may differ from the reference program's by a relative error of at most 0.007.
Values may be sent and summed in bfloat16 or wider, within the bound.
A program may use at most 128 MiB of HBM per device.

```python
import math
import jax
import jax.numpy as jnp
from jax import lax

C0 = 4
C1 = 32
C2 = 64
DZ = 4
PLANE = 128
BATCH = 2
NZ = 256
K1 = 108
K2 = 864
N_SPACE = 64


def draw_volume(key, part):
    key = jax.random.fold_in(key, 11)
    noise_key, plane_key, column_key = jax.random.split(key, 3)
    full_shape = (C0, BATCH, NZ, PLANE, PLANE)
    plane_scale = jnp.exp(jax.random.uniform(plane_key, (C0, BATCH, NZ, 1, 1), jnp.float32, math.log(0.3), math.log(3.0)))
    column_scale = jnp.exp(jax.random.uniform(column_key, (C0, 1, 1, 1, PLANE), jnp.float32, math.log(0.5), math.log(2.0)))
    rising = jnp.exp(math.log(3.0) * jnp.arange(NZ, dtype=jnp.float32) / (NZ - 1)).reshape(1, 1, NZ, 1, 1)
    values_raw = jax.random.truncated_normal(noise_key, -4.0, 4.0, full_shape, jnp.float32)
    return (values_raw * plane_scale * rising * column_scale).astype(jnp.bfloat16)


def steps_of(rng, extent, shards, low, largest):
    def one(axis_at, parts):
        heights = jax.random.uniform(jax.random.fold_in(jax.random.fold_in(rng, 6), axis_at), (parts,), jnp.float32, low / len(shards), largest / len(shards))
        return jnp.repeat(jnp.exp(heights), extent[axis_at] // parts).reshape((-1,) + (1,) * (len(extent) - axis_at - 1))

    level = one(*shards[0])
    for cut in shards[1:]:
        level = level * one(*cut)
    return level


def gaussian(key, extent, spread, limit, cuts=(), kind=jnp.bfloat16):
    level = steps_of(key, extent, cuts, -0.22, 0.18) if cuts else 1.0
    entries = jax.random.normal(key, extent, jnp.float32) * spread * level
    return jnp.minimum(jnp.maximum(entries, -limit), limit).astype(kind)


def setup_inputs(seed: int = 0) -> dict:
    seeds = jax.random.split(jax.random.key(seed), 5)
    return {
        "volume": draw_volume(jax.random.fold_in(seeds[4], 71), 0),
        "kernel_one": gaussian(seeds[1], (K1, C1), K1 ** -0.5, 0.625),
        "kernel_two": gaussian(seeds[2], (K2, C2), K2 ** -0.5, 0.21875),
        "cotangent": gaussian(seeds[3], (C2, BATCH, NZ // 4, (PLANE // 4) * (PLANE // 4)), 1.0, 6.0, ((1, 2), (2, 64))),
    }


def gelu_slope(value):
    inner = 0.7978845608028654 * (value + 0.044715 * value * value * value)
    tangent = jnp.tanh(inner)
    return 0.5 * (1.0 + tangent) + 0.5 * value * (1.0 - tangent * tangent) * 0.7978845608028654 * (1.0 + 3.0 * 0.044715 * value * value)

def build_patches(padded):
    plane_count = (padded.shape[2] - 1) // 2
    row_count = (padded.shape[3] - 1) // 2
    col_count = (padded.shape[4] - 1) // 2
    pieces = []
    for depth_off in range(3):
        for row_off in range(3):
            for col_off in range(3):
                pieces.append(padded[:, :, depth_off:depth_off + 2 * plane_count:2, row_off:row_off + 2 * row_count:2, col_off:col_off + 2 * col_count:2])
    return jnp.stack(pieces, axis=1).reshape(padded.shape[0] * 27, -1)

def gram(first_op, second_op):
    return lax.dot_general(first_op, second_op, (((1,), (1,)), ((), ())), preferred_element_type=jnp.float32)

def convolve(field, kernel):
    kernel_taps = kernel.astype(jnp.float32).reshape(field.shape[0], 3, 3, 3, kernel.shape[1])
    return lax.conv_general_dilated(field.astype(jnp.float32), kernel_taps, (2, 2, 2), ((1, 0), (1, 0), (1, 0)), dimension_numbers=('CNDHW', 'IDHWO', 'CNDHW'), precision=lax.Precision.HIGHEST)

def full_margin(field):
    return jnp.pad(field, ((0, 0), (0, 0), (1, 0), (1, 0), (1, 0)))

def factor_sums(padded, grads, plane_block, blocks):
    rows_k = padded.shape[0] * 27
    grad_chan = grads.shape[0]

    def accumulate(block_index, totals):
        first_plane = (block_index * (2 * plane_block)).astype(jnp.int32)
        slab = lax.dynamic_slice_in_dim(padded, first_plane, 2 * plane_block + 1, axis=2)
        patches = build_patches(slab)
        grad_first = (block_index * plane_block).astype(jnp.int32)
        grad_block = lax.dynamic_slice_in_dim(grads, grad_first, plane_block, axis=2).reshape(grad_chan, -1)
        return (totals[0] + gram(patches, patches), totals[1] + gram(grad_block, grad_block), totals[2] + gram(patches, grad_block))
    initial = (jnp.zeros((rows_k, rows_k), jnp.float32), jnp.zeros((grad_chan, grad_chan), jnp.float32), jnp.zeros((rows_k, grad_chan), jnp.float32))
    return lax.fori_loop(0, blocks, accumulate, initial)

def reference(volume, kernel_one, kernel_two, cotangent):
    pre_one = convolve(volume, kernel_one)
    hidden = jax.nn.gelu(pre_one, approximate=True).astype(jnp.bfloat16)
    pre_two, pullback = jax.vjp(lambda field: convolve(field, kernel_two), hidden.astype(jnp.float32))
    features = jax.nn.gelu(pre_two, approximate=True).astype(jnp.bfloat16).reshape(C2, BATCH, NZ // 4, -1)
    total_one = BATCH * (NZ // 2) * (PLANE // 2) * (PLANE // 2)
    total_two = BATCH * (NZ // 4) * (PLANE // 4) * (PLANE // 4)
    cot_field = cotangent.reshape(C2, BATCH, NZ // 4, PLANE // 4, PLANE // 4).astype(jnp.float32)
    grad_two = (cot_field * (1.0 / math.sqrt(total_two)) * gelu_slope(pre_two)).astype(jnp.bfloat16)
    grad_hidden = pullback(grad_two.astype(jnp.float32))[0]
    grad_one = (grad_hidden * gelu_slope(pre_one)).astype(jnp.bfloat16)
    in_one, out_one, weight_one = factor_sums(full_margin(volume), grad_one, DZ // 2, N_SPACE)
    in_two, out_two, weight_two = factor_sums(full_margin(hidden), grad_two, DZ // 4, N_SPACE)
    return (features, in_one / total_one, in_two / total_two, out_one, out_two, weight_one, weight_two)
```

```python
import math

import jax
import jax.numpy as jnp
import numpy as np
from jax import lax
from jax.experimental import pallas as pl
from jax.experimental.pallas import tpu as pltpu
from jax.sharding import PartitionSpec as P

F32 = jnp.float32
BF16 = jnp.bfloat16
VMEM_CAP = 56 * 1024 * 1024
TOTAL_ONE = 2 * 128 * 64 * 64
TOTAL_TWO = 2 * 64 * 32 * 32


def spread_matrix():
    table = np.zeros((4, 128, 5, 4, 32), np.float32)
    for m in range(4):
        for res in range(5):
            for x2 in range(32):
                x = 4 * x2 + res - 1
                if x >= 0:
                    table[m, x, res, m, x2] = 1
    return jnp.asarray(table.reshape(512, 640), BF16)


def tap_matrix():
    table = np.zeros((128, 4, 3, 128), np.float32)
    for p in range(2):
        for q in range(2):
            for c in range(4):
                for a in range(3):
                    for b in range(3):
                        for e in range(3):
                            row = c * 27 + a * 9 + b * 3 + e
                            table[row, p * 2 + q, a, (2 * q + e) * 20 + c * 5 + 2 * p + b] = 1
    return jnp.asarray(table.reshape(128, 1536), BF16)


def gelu_parts(value):
    square = value * value
    tangent = jnp.tanh(0.7978845608028654 * (value + 0.044715 * value * square))
    half = 0.5 * (1.0 + tangent)
    slope = half + 0.5 * value * (1.0 - tangent * tangent) * 0.7978845608028654 * (1.0 + 3.0 * 0.044715 * square)
    return value * half, slope


def dot(a, b):
    return lax.dot_general(a, b, (((1,), (0,)), ((), ())), preferred_element_type=F32)


def dot_nt(a, b):
    return lax.dot_general(a, b, (((1,), (1,)), ((), ())), preferred_element_type=F32)


def halves(value):
    high = value.astype(BF16)
    return high, (value - high.astype(F32)).astype(BF16)


def forward_kernel(
    vol_ref, rim_ref, k1_ref, k2_ref, cot_ref, spread_ref, tap_ref,
    sums_ref, feat_ref, g2_ref, u_ref, slope_ref,
    vf, lf, of, uu, k1p, ww, p2f, p2b, tiles,
):
    lane = lax.broadcasted_iota(jnp.int32, (1, 1024), 1)
    for zz in range(7):
        for c in range(4):
            plane = rim_ref[c, 0, zz] if zz < 3 else vol_ref[c, 0, zz - 3]
            vf[zz * 4 + c, 8:136, :] = plane.astype(F32)
            vf[zz * 4 + c, 0:8, :] = jnp.zeros((8, 128), F32)
    for plane in range(28):
        for res in range(5):
            for m in range(4):
                row = (plane * 5 + res) * 8
                lf[row : row + 8, m * 128 : (m + 1) * 128] = vf[plane, pl.ds(7 + 4 * m + res, 8, stride=16), :]
    spread = dot(lf[...].astype(BF16), spread_ref[...])
    for zz in range(7):
        for res in range(5):
            of[zz * 1024 + res * 160 : zz * 1024 + (res + 1) * 160, :] = spread[
                zz * 160 : (zz + 1) * 160, res * 128 : (res + 1) * 128
            ]
        of[zz * 1024 + 800 : zz * 1024 + 896, :] = jnp.zeros((96, 128), F32)
    for zz in range(7):
        for group in range(7):
            for j in range(8):
                start = zz * 1024 + group * 128 + j
                part = jnp.concatenate(
                    [of[pl.ds(start, 8, stride=8), :], of[pl.ds(start + 64, 8, stride=8), :]], axis=0
                )
                uu[zz * 128 + group * 16 : zz * 128 + (group + 1) * 16, j * 128 : (j + 1) * 128] = part.astype(BF16)
        uu[zz * 128 + 112 : zz * 128 + 128, :] = jnp.zeros((16, 1024), BF16)
    u_ref[...] = uu[256:896, :]

    k1p[...] = jnp.zeros((32, 128), BF16)
    k1p[:, 0:108] = k1_ref[...]
    wide = dot(k1p[...], tap_ref[...])
    for pq in range(4):
        ww[pq * 32 : (pq + 1) * 32, :] = wide[:, pq * 384 : (pq + 1) * 384].astype(BF16)

    for h in range(3):
        pre = dot(ww[...], uu[h * 256 : h * 256 + 384, :])
        act, slope = gelu_parts(pre)
        if h > 0:
            slope_ref[(h - 1) * 128 : h * 128, :] = slope
        act = act.astype(BF16).astype(F32)
        for b in range(3):
            for e in range(3):
                p, q = (b + 1) % 2, (e + 1) % 2
                block = act[(p * 2 + q) * 32 : (p * 2 + q + 1) * 32, :]
                if e == 0:
                    block = jnp.where(lane % 32 == 0, 0.0, pltpu.roll(block, 1, 1))
                if b == 0:
                    block = jnp.where(lane < 32, 0.0, pltpu.roll(block, 32, 1))
                tap = h * 9 + b * 3 + e
                for j in range(8):
                    p2f[j, pl.ds(tap, 32, stride=27), :] = block[:, j * 128 : (j + 1) * 128]
    for j in range(8):
        p2b[0:864, j * 128 : (j + 1) * 128] = p2f[j].astype(BF16)
    p2b[864:896, :] = jnp.zeros((32, 1024), BF16)
    p2b[896:1280, :] = p2b[0:384, :]

    pre_two = dot(k2_ref[...], p2b[0:864, :])
    act, slope = gelu_parts(pre_two)
    act = act.astype(BF16).astype(F32)
    g2 = (cot_ref[...].astype(F32) * (1.0 / math.sqrt(TOTAL_TWO)) * slope).astype(BF16)
    g2_ref[...] = g2

    chan = lax.broadcasted_iota(jnp.int32, (64, 1024), 0) % 8
    group = (lax.broadcasted_iota(jnp.int32, (64, 1024), 1) // 16) % 8
    for bit in (4, 2, 1):
        down = pltpu.roll(pltpu.roll(act, 64 - bit, 0), bit * 16, 1)
        up = pltpu.roll(pltpu.roll(act, bit, 0), 1024 - bit * 16, 1)
        in_chan = (chan & bit) != 0
        in_group = (group & bit) != 0
        act = jnp.where(in_chan == in_group, act, jnp.where(in_group, down, up))
    for r in range(8):
        for g in range(8):
            feat_ref[pl.ds(64 * g + r, 8, stride=8), :] = act[r * 8 : (r + 1) * 8, g * 128 : (g + 1) * 128]

    for i in range(7):
        block = dot_nt(p2b[i * 128 : (i + 1) * 128, :], p2b[i * 128 : i * 128 + 512, :]) * (1.0 / TOTAL_TWO)
        sums_ref[i * 128 : (i + 1) * 128, :] = block.astype(BF16)
    grads = dot_nt(g2, p2b[0:896, :])
    own = dot_nt(g2, g2)
    sums_ref[896:960, :] = grads[:, 0:512].astype(BF16)
    sums_ref[960:1024, 0:384] = grads[:, 512:896].astype(BF16)
    sums_ref[960:1024, 384:512] = jnp.concatenate([own, jnp.zeros((64, 64), F32)], axis=1).astype(BF16)
    gram = dot_nt(uu[256:640, :], uu[256:640, :]) + dot_nt(uu[512:896, :], uu[512:896, :])
    total = jnp.zeros((128, 128), F32)
    for part in halves(gram):
        for pq in range(4):
            taps = tap_ref[:, pq * 384 : (pq + 1) * 384]
            total = total + dot(taps, dot_nt(part, taps).astype(BF16))
    total = total * (1.0 / TOTAL_ONE)
    for k in range(4):
        tiles[:, k * 128 : (k + 1) * 128] = total[k * 32 : (k + 1) * 32, :]
    sums_ref[864:896, :] = tiles[...].astype(BF16)


def backward_kernel(u_ref, slope_ref, g2_ref, above_ref, k2_ref, tap_ref, late_ref, k2f, aa, gs):
    lane = lax.broadcasted_iota(jnp.int32, (1, 1024), 1)
    k2f[:, 0:64] = k2_ref[...].astype(F32).T
    aa[...] = jnp.zeros((3, 128, 256), BF16)
    for a in range(3):
        for b in range(3):
            for e in range(3):
                p, q = (b + 1) % 2, (e + 1) % 2
                sy, sx = int(b == 0), int(e == 0)
                block = k2f[pl.ds(a * 9 + b * 3 + e, 32, stride=27), :]
                at = (p * 2 + q) * 32
                aa[a, at : at + 32, (sy * 2 + sx) * 64 : (sy * 2 + sx + 1) * 64] = block[:, 0:64].astype(BF16)
    for n, ref in enumerate((g2_ref, above_ref)):
        for sy in range(2):
            for sx in range(2):
                moved = ref[...].astype(F32)
                if sx:
                    moved = jnp.where(lane % 32 == 31, 0.0, pltpu.roll(moved, 1023, 1))
                if sy:
                    moved = jnp.where(lane >= 992, 0.0, pltpu.roll(moved, 992, 1))
                gs[n, (sy * 2 + sx) * 64 : (sy * 2 + sx + 1) * 64, :] = moved.astype(BF16)
    cross = jnp.zeros((128, 384), F32)
    gram = jnp.zeros((128, 128), F32)
    for h in range(2):
        spread = dot(aa[h + 1], gs[0])
        if h == 1:
            spread = spread + dot(aa[0], gs[1])
        g1 = (spread * slope_ref[h * 128 : (h + 1) * 128, :]).astype(BF16)
        cross = cross + dot_nt(g1, u_ref[h * 256 : h * 256 + 384, :])
        gram = gram + dot_nt(g1, g1)
    weight = jnp.zeros((32, 128), F32)
    own = jnp.zeros((32, 32), F32)
    for pq in range(4):
        for part in halves(cross[pq * 32 : (pq + 1) * 32, :]):
            weight = weight + dot_nt(part, tap_ref[:, pq * 384 : (pq + 1) * 384])
        own = own + gram[pq * 32 : (pq + 1) * 32, pq * 32 : (pq + 1) * 32]
    late_ref[:, 0:128] = weight
    late_ref[:, 128:256] = jnp.concatenate([own, jnp.zeros((32, 96), F32)], axis=1)


def unpack_kernel(
    sums_ref, late_ref, feat_ref,
    features_ref, in_one_ref, in_two_ref, out_one_ref, out_two_ref, w_one_ref, w_two_ref,
):
    for i in range(7):
        rows = min(128, 864 - i * 128)
        for k in range(4):
            j = (i + k) % 7
            cols = min(128, 864 - j * 128)
            block = sums_ref[i * 128 : (i + 1) * 128, k * 128 : (k + 1) * 128].astype(F32)
            in_two_ref[i * 128 : i * 128 + rows, j * 128 : j * 128 + cols] = block[0:rows, 0:cols]
            if k:
                in_two_ref[j * 128 : j * 128 + cols, i * 128 : i * 128 + rows] = block.T[0:cols, 0:rows]
    w_two_ref[:, 0:512] = sums_ref[896:960, :].astype(F32)
    rest = sums_ref[960:1024, :].astype(F32)
    w_two_ref[:, 512:864] = rest[:, 0:352]
    out_two_ref[...] = rest[:, 384:448]
    first = sums_ref[864:896, :].astype(F32)
    for k in range(4):
        rows = min(32, 108 - k * 32)
        in_one_ref[k * 32 : k * 32 + rows, :] = first[0:rows, k * 128 : k * 128 + 108]
    late = late_ref[...]
    w_one_ref[...] = late[:, 0:108]
    out_one_ref[...] = late[:, 128:160]
    for r in range(8):
        block = feat_ref[pl.ds(r, 64, stride=8), :]
        features_ref[r * 8 : (r + 1) * 8, 0, :, :] = block.T.reshape(8, 16, 64).astype(BF16)


VM = pl.BlockSpec(memory_space=pltpu.VMEM)


def passed_along(block, axis, distance):
    devices = range(lax.axis_size(axis))
    route = [(i - distance, i) for i in devices if i - distance in devices]
    return lax.ppermute(block, axis, route)


def local(volume, kernel_one, kernel_two, cotangent):
    shape = jax.ShapeDtypeStruct
    spread, taps = spread_matrix(), tap_matrix()
    rim = passed_along(volume[:, :, 1:], "space", 1)
    sums, feat, g2, uu, slope = pl.pallas_call(
        forward_kernel,
        name="forward",
        out_shape=(
            shape((1024, 512), BF16), shape((512, 128), F32), shape((64, 1024), BF16),
            shape((640, 1024), BF16), shape((256, 1024), F32),
        ),
        in_specs=[VM] * 7,
        out_specs=(VM,) * 5,
        scratch_shapes=[
            pltpu.VMEM((28, 136, 128), F32),
            pltpu.VMEM((1120, 512), F32),
            pltpu.VMEM((7 * 1024, 128), F32),
            pltpu.VMEM((896, 1024), BF16),
            pltpu.VMEM((32, 128), BF16),
            pltpu.VMEM((128, 384), BF16),
            pltpu.VMEM((8, 864, 128), F32),
            pltpu.VMEM((1280, 1024), BF16),
            pltpu.VMEM((32, 512), F32),
        ],
        compiler_params=pltpu.CompilerParams(vmem_limit_bytes=VMEM_CAP),
    )(volume, rim, kernel_one.T, kernel_two.T, cotangent.reshape(64, 1024), spread, taps)
    above = passed_along(g2, "space", -1)
    late = pl.pallas_call(
        backward_kernel,
        name="backward",
        out_shape=shape((32, 256), F32),
        in_specs=[VM] * 6,
        out_specs=VM,
        scratch_shapes=[
            pltpu.VMEM((864, 128), F32),
            pltpu.VMEM((3, 128, 256), BF16),
            pltpu.VMEM((2, 256, 1024), BF16),
        ],
        compiler_params=pltpu.CompilerParams(vmem_limit_bytes=VMEM_CAP),
    )(uu, slope, g2, above, kernel_two.T, taps)
    feat = lax.all_to_all(feat, "space", split_axis=0, concat_axis=0, tiled=True)
    late, sums = lax.psum((late, sums.astype(F32)), ("space", "batch"))
    features, in_one, in_two, out_one, out_two, w_one, w_two = pl.pallas_call(
        unpack_kernel,
        name="unpack",
        out_shape=(
            shape((64, 1, 16, 64), BF16), shape((108, 108), F32), shape((864, 864), F32), shape((32, 32), F32),
            shape((64, 64), F32), shape((32, 108), F32), shape((64, 864), F32),
        ),
        in_specs=[VM] * 3,
        out_specs=(VM,) * 7,
        compiler_params=pltpu.CompilerParams(vmem_limit_bytes=VMEM_CAP),
    )(sums, late, feat)
    return features.transpose(0, 1, 3, 2), in_one, in_two, out_one, out_two, w_one.T, w_two.T


def solution(mesh):
    placed = (P(None, "batch", "space", None, None), P(), P(), P(None, "batch", "space", None))
    return jax.shard_map(
        local,
        mesh=mesh,
        in_specs=placed,
        out_specs=(P(None, "batch", None, "space"), P(), P(), P(), P(), P(), P()),
        check_vma=False,
    )
```

```python
import math

import jax
import jax.numpy as jnp
import numpy as np
from jax import lax
from jax.experimental import pallas as pl
from jax.experimental.pallas import tpu as pltpu
from jax.sharding import PartitionSpec as P

F32 = jnp.float32
BF16 = jnp.bfloat16
VMEM_CAP = 56 * 1024 * 1024
TOTAL_ONE = 2 * 128 * 64 * 64
TOTAL_TWO = 2 * 64 * 32 * 32


def spread_matrix():
    table = np.zeros((4, 128, 5, 4, 32), np.float32)
    for m in range(4):
        for res in range(5):
            for x2 in range(32):
                x = 4 * x2 + res - 1
                if x >= 0:
                    table[m, x, res, m, x2] = 1
    return jnp.asarray(table.reshape(512, 640), BF16)


def tap_matrix():
    table = np.zeros((128, 4, 3, 128), np.float32)
    for p in range(2):
        for q in range(2):
            for c in range(4):
                for a in range(3):
                    for b in range(3):
                        for e in range(3):
                            row = c * 27 + a * 9 + b * 3 + e
                            table[row, p * 2 + q, a, (2 * q + e) * 20 + c * 5 + 2 * p + b] = 1
    return jnp.asarray(table.reshape(128, 1536), BF16)


def gelu_parts(value):
    square = value * value
    tangent = jnp.tanh(0.7978845608028654 * (value + 0.044715 * value * square))
    half = 0.5 * (1.0 + tangent)
    slope = half + 0.5 * value * (1.0 - tangent * tangent) * 0.7978845608028654 * (1.0 + 3.0 * 0.044715 * square)
    return value * half, slope


def dot(a, b):
    return lax.dot_general(a, b, (((1,), (0,)), ((), ())), preferred_element_type=F32)


def dot_nt(a, b):
    return lax.dot_general(a, b, (((1,), (1,)), ((), ())), preferred_element_type=F32)


def halves(value):
    high = value.astype(BF16)
    return high, (value - high.astype(F32)).astype(BF16)


def forward_kernel(
    vol_ref, rim_ref, k1_ref, k2_ref, cot_ref, spread_ref, tap_ref,
    sums_ref, feat_ref, g2_ref, u_ref, slope_ref,
    vf, lf, of, uu, k1p, ww, p2f, p2b, tiles,
):
    lane = lax.broadcasted_iota(jnp.int32, (1, 1024), 1)
    for zz in range(7):
        for c in range(4):
            plane = rim_ref[c, 0, zz] if zz < 3 else vol_ref[c, 0, zz - 3]
            vf[zz * 4 + c, 8:136, :] = plane.astype(F32)
            vf[zz * 4 + c, 0:8, :] = jnp.zeros((8, 128), F32)
    for plane in range(28):
        for res in range(5):
            for m in range(4):
                row = (plane * 5 + res) * 8
                lf[row : row + 8, m * 128 : (m + 1) * 128] = vf[plane, pl.ds(7 + 4 * m + res, 8, stride=16), :]
    spread = dot(lf[...].astype(BF16), spread_ref[...])
    for zz in range(7):
        for res in range(5):
            of[zz * 1024 + res * 160 : zz * 1024 + (res + 1) * 160, :] = spread[
                zz * 160 : (zz + 1) * 160, res * 128 : (res + 1) * 128
            ]
        of[zz * 1024 + 800 : zz * 1024 + 896, :] = jnp.zeros((96, 128), F32)
    for zz in range(7):
        for group in range(7):
            for j in range(8):
                start = zz * 1024 + group * 128 + j
                part = jnp.concatenate(
                    [of[pl.ds(start, 8, stride=8), :], of[pl.ds(start + 64, 8, stride=8), :]], axis=0
                )
                uu[zz * 128 + group * 16 : zz * 128 + (group + 1) * 16, j * 128 : (j + 1) * 128] = part.astype(BF16)
        uu[zz * 128 + 112 : zz * 128 + 128, :] = jnp.zeros((16, 1024), BF16)
    u_ref[...] = uu[256:896, :]

    k1p[...] = jnp.zeros((32, 128), BF16)
    k1p[:, 0:108] = k1_ref[...]
    wide = dot(k1p[...], tap_ref[...])
    for pq in range(4):
        ww[pq * 32 : (pq + 1) * 32, :] = wide[:, pq * 384 : (pq + 1) * 384].astype(BF16)

    for h in range(3):
        pre = dot(ww[...], uu[h * 256 : h * 256 + 384, :])
        act, slope = gelu_parts(pre)
        if h > 0:
            slope_ref[(h - 1) * 128 : h * 128, :] = slope
        act = act.astype(BF16).astype(F32)
        for b in range(3):
            for e in range(3):
                p, q = (b + 1) % 2, (e + 1) % 2
                block = act[(p * 2 + q) * 32 : (p * 2 + q + 1) * 32, :]
                if e == 0:
                    block = jnp.where(lane % 32 == 0, 0.0, pltpu.roll(block, 1, 1))
                if b == 0:
                    block = jnp.where(lane < 32, 0.0, pltpu.roll(block, 32, 1))
                tap = h * 9 + b * 3 + e
                for j in range(8):
                    p2f[j, pl.ds(tap, 32, stride=27), :] = block[:, j * 128 : (j + 1) * 128]
    for j in range(8):
        p2b[0:864, j * 128 : (j + 1) * 128] = p2f[j].astype(BF16)
    p2b[864:896, :] = jnp.zeros((32, 1024), BF16)
    p2b[896:1280, :] = p2b[0:384, :]

    pre_two = dot(k2_ref[...], p2b[0:864, :])
    act, slope = gelu_parts(pre_two)
    act = act.astype(BF16).astype(F32)
    g2 = (cot_ref[...].astype(F32) * (1.0 / math.sqrt(TOTAL_TWO)) * slope).astype(BF16)
    g2_ref[...] = g2

    chan = lax.broadcasted_iota(jnp.int32, (64, 1024), 0) % 8
    group = (lax.broadcasted_iota(jnp.int32, (64, 1024), 1) // 16) % 8
    for bit in (4, 2, 1):
        down = pltpu.roll(pltpu.roll(act, 64 - bit, 0), bit * 16, 1)
        up = pltpu.roll(pltpu.roll(act, bit, 0), 1024 - bit * 16, 1)
        in_chan = (chan & bit) != 0
        in_group = (group & bit) != 0
        act = jnp.where(in_chan == in_group, act, jnp.where(in_group, down, up))
    for r in range(8):
        for g in range(8):
            feat_ref[pl.ds(64 * g + r, 8, stride=8), :] = act[r * 8 : (r + 1) * 8, g * 128 : (g + 1) * 128]

    for i in range(7):
        block = dot_nt(p2b[i * 128 : (i + 1) * 128, :], p2b[i * 128 : i * 128 + 512, :]) * (1.0 / TOTAL_TWO)
        sums_ref[i * 128 : (i + 1) * 128, :] = block.astype(BF16)
    grads = dot_nt(g2, p2b[0:896, :])
    own = dot_nt(g2, g2)
    sums_ref[896:960, :] = grads[:, 0:512].astype(BF16)
    sums_ref[960:1024, 0:384] = grads[:, 512:896].astype(BF16)
    sums_ref[960:1024, 384:512] = jnp.concatenate([own, jnp.zeros((64, 64), F32)], axis=1).astype(BF16)
    gram = dot_nt(uu[256:640, :], uu[256:640, :]) + dot_nt(uu[512:896, :], uu[512:896, :])
    total = jnp.zeros((128, 128), F32)
    for part in halves(gram):
        for pq in range(4):
            taps = tap_ref[:, pq * 384 : (pq + 1) * 384]
            total = total + dot(taps, dot_nt(part, taps).astype(BF16))
    total = total * (1.0 / TOTAL_ONE)
    for k in range(4):
        tiles[:, k * 128 : (k + 1) * 128] = total[k * 32 : (k + 1) * 32, :]
    sums_ref[864:896, :] = tiles[...].astype(BF16)


def backward_kernel(u_ref, slope_ref, g2_ref, above_ref, k2_ref, tap_ref, late_ref, k2f, aa, gs):
    lane = lax.broadcasted_iota(jnp.int32, (1, 1024), 1)
    k2f[:, 0:64] = k2_ref[...].astype(F32).T
    aa[...] = jnp.zeros((3, 128, 256), BF16)
    for a in range(3):
        for b in range(3):
            for e in range(3):
                p, q = (b + 1) % 2, (e + 1) % 2
                sy, sx = int(b == 0), int(e == 0)
                block = k2f[pl.ds(a * 9 + b * 3 + e, 32, stride=27), :]
                at = (p * 2 + q) * 32
                aa[a, at : at + 32, (sy * 2 + sx) * 64 : (sy * 2 + sx + 1) * 64] = block[:, 0:64].astype(BF16)
    for n, ref in enumerate((g2_ref, above_ref)):
        for sy in range(2):
            for sx in range(2):
                moved = ref[...].astype(F32)
                if sx:
                    moved = jnp.where(lane % 32 == 31, 0.0, pltpu.roll(moved, 1023, 1))
                if sy:
                    moved = jnp.where(lane >= 992, 0.0, pltpu.roll(moved, 992, 1))
                gs[n, (sy * 2 + sx) * 64 : (sy * 2 + sx + 1) * 64, :] = moved.astype(BF16)
    cross = jnp.zeros((128, 384), F32)
    gram = jnp.zeros((128, 128), F32)
    for h in range(2):
        spread = dot(aa[h + 1], gs[0])
        if h == 1:
            spread = spread + dot(aa[0], gs[1])
        g1 = (spread * slope_ref[h * 128 : (h + 1) * 128, :]).astype(BF16)
        cross = cross + dot_nt(g1, u_ref[h * 256 : h * 256 + 384, :])
        gram = gram + dot_nt(g1, g1)
    weight = jnp.zeros((32, 128), F32)
    own = jnp.zeros((32, 32), F32)
    for pq in range(4):
        for part in halves(cross[pq * 32 : (pq + 1) * 32, :]):
            weight = weight + dot_nt(part, tap_ref[:, pq * 384 : (pq + 1) * 384])
        own = own + gram[pq * 32 : (pq + 1) * 32, pq * 32 : (pq + 1) * 32]
    late_ref[:, 0:128] = weight
    late_ref[:, 128:256] = jnp.concatenate([own, jnp.zeros((32, 96), F32)], axis=1)


def unpack_kernel(
    sums_ref, late_ref, feat_ref,
    features_ref, in_one_ref, in_two_ref, out_one_ref, out_two_ref, w_one_ref, w_two_ref,
):
    for i in range(7):
        rows = min(128, 864 - i * 128)
        for k in range(4):
            j = (i + k) % 7
            cols = min(128, 864 - j * 128)
            block = sums_ref[i * 128 : (i + 1) * 128, k * 128 : (k + 1) * 128].astype(F32)
            in_two_ref[i * 128 : i * 128 + rows, j * 128 : j * 128 + cols] = block[0:rows, 0:cols]
            if k:
                in_two_ref[j * 128 : j * 128 + cols, i * 128 : i * 128 + rows] = block.T[0:cols, 0:rows]
    w_two_ref[:, 0:512] = sums_ref[896:960, :].astype(F32)
    rest = sums_ref[960:1024, :].astype(F32)
    w_two_ref[:, 512:864] = rest[:, 0:352]
    out_two_ref[...] = rest[:, 384:448]
    first = sums_ref[864:896, :].astype(F32)
    for k in range(4):
        rows = min(32, 108 - k * 32)
        in_one_ref[k * 32 : k * 32 + rows, :] = first[0:rows, k * 128 : k * 128 + 108]
    late = late_ref[...]
    w_one_ref[...] = late[:, 0:108]
    out_one_ref[...] = late[:, 128:160]
    for r in range(8):
        block = feat_ref[pl.ds(r, 64, stride=8), :]
        features_ref[r * 8 : (r + 1) * 8, 0, :, :] = block.T.reshape(8, 16, 64).astype(BF16)


VM = pl.BlockSpec(memory_space=pltpu.VMEM)
MESH = pl.DeviceIdType.MESH


def shifted(me, k):
    y = lax.rem(me // 16 + k // 16, 4)
    z = lax.rem(lax.rem(me // 4, 4) + lax.rem(k // 4, 4), 4)
    x = lax.rem(lax.rem(me, 4) + lax.rem(k, 4), 4)
    return y * 16 + z * 4 + x


def sum_kernel(
    sums_ref, late_ref, feat_ref, out_ref, late_out_ref, feat_out_ref,
    pair, half, got, late_pair, late_x, late_sum, late_yz, late_total,
    pair_sem, late_pair_sem, rs_sem, feat_sem, x_sem, yz_sem, gather_send, gather_recv, back_sem,
):
    me, core = lax.axis_index("space"), lax.axis_index("batch")
    sibling = (me, 1 - core)
    mine = pl.ds(pl.multiple_of(core * 256, 256), 256)
    other = pl.ds(pl.multiple_of((1 - core) * 256, 256), 256)

    def rows(index):
        return pl.ds(pl.multiple_of(index * 16, 16), 16)

    def send(src, dst, sems, to):
        copy = pltpu.make_async_remote_copy(
            src_ref=src, dst_ref=dst, send_sem=sems.at[0], recv_sem=sems.at[1], device_id=to, device_id_type=MESH
        )
        copy.start()
        return copy

    def await_bytes(ref, sem):
        pltpu.make_async_copy(ref, ref, sem).wait()

    barrier = pltpu.get_barrier_semaphore()
    pl.semaphore_signal(barrier, inc=1, device_id=sibling, device_id_type=MESH)

    def greet(k, carry):
        pl.semaphore_signal(barrier, inc=1, device_id=(shifted(me, k), core), device_id_type=MESH)
        return carry

    lax.fori_loop(1, 64, greet, 0)
    pl.semaphore_wait(barrier, 64)

    pair_copy = send(sums_ref.at[:, other], pair, pair_sem, sibling)
    late_copy = send(late_ref, late_pair, late_pair_sem, sibling)
    pair_copy.wait()
    half[...] = (sums_ref[:, mine].astype(F32) + pair[...].astype(F32)).astype(BF16)

    def scatter(k, carry):
        to = shifted(me, k)
        send(half.at[rows(to), :], got.at[rows(k - 1), :], rs_sem, (to, core))
        return carry

    lax.fori_loop(1, 64, scatter, 0)

    late_copy.wait()
    late_sum[...] = late_ref[...] + late_pair[...]

    def along_x(k, carry):
        send(late_sum, late_x.at[k - 1], x_sem, (shifted(me, k), core))
        return carry

    lax.fori_loop(1, 4, along_x, 0)

    def hand_on(k, carry):
        to = shifted(me, k)
        there = pl.ds(pl.multiple_of(to * 8, 8), 8)
        here = pl.ds(pl.multiple_of(me * 8, 8), 8)
        send(feat_ref.at[there, :], feat_out_ref.at[here, :], feat_sem, (to, core))
        return carry

    lax.fori_loop(1, 64, hand_on, 0)

    await_bytes(late_x, x_sem.at[0])
    await_bytes(late_x, x_sem.at[1])
    late_total[...] = late_sum[...] + (late_x[0] + late_x[1] + late_x[2])

    def across(k, carry):
        send(late_total, late_yz.at[k - 1], yz_sem, (shifted(me, 4 * k), core))
        return carry

    lax.fori_loop(1, 16, across, 0)

    await_bytes(got, rs_sem.at[1])

    def add(k, total):
        return total + got[rows(k), :].astype(F32)

    total = lax.fori_loop(0, 63, add, half[rows(me), :].astype(F32))
    out_ref[rows(me), mine] = total.astype(BF16)

    def gather(k, carry):
        piece = out_ref.at[rows(me), mine]
        copy = pltpu.make_async_remote_copy(
            src_ref=piece, dst_ref=piece, send_sem=gather_send, recv_sem=gather_recv.at[k // 16],
            device_id=(shifted(me, k), core), device_id_type=MESH,
        )
        copy.start()
        return carry

    lax.fori_loop(1, 64, gather, 0)

    await_bytes(late_yz, yz_sem.at[0])
    await_bytes(late_yz, yz_sem.at[1])
    late_out_ref[...] = lax.fori_loop(0, 15, lambda k, total: total + late_yz[k], late_total[...])
    feat_out_ref[pl.ds(pl.multiple_of(me * 8, 8), 8), :] = feat_ref[pl.ds(pl.multiple_of(me * 8, 8), 8), :]

    backs = []
    for k in range(4):
        count = 240 if k == 0 else 256
        await_bytes(half.at[0:count, :], gather_recv.at[k])
        block = pl.ds(pl.multiple_of(lax.rem(me // 16 + 4 - k, 4) * 256, 256), 256)
        backs.append(send(out_ref.at[block, mine], out_ref.at[block, mine], back_sem.at[k], sibling))
    for copy in backs:
        copy.wait()
    await_bytes(got, rs_sem.at[0])
    await_bytes(got, gather_send)
    for sem in (feat_sem.at[0], feat_sem.at[1]):
        await_bytes(feat_out_ref.at[0:504, :], sem)


def summed(sums, late, feat):
    shape = jax.ShapeDtypeStruct
    dma = pltpu.SemaphoreType.DMA
    return pl.pallas_call(
        sum_kernel,
        name="summed",
        out_shape=(shape((1024, 512), BF16), shape((32, 256), F32), shape((512, 128), F32)),
        in_specs=[VM] * 3,
        out_specs=(VM,) * 3,
        scratch_shapes=[
            pltpu.VMEM((1024, 256), BF16),
            pltpu.VMEM((1024, 256), BF16),
            pltpu.VMEM((1008, 256), BF16),
            pltpu.VMEM((32, 256), F32),
            pltpu.VMEM((3, 32, 256), F32),
            pltpu.VMEM((32, 256), F32),
            pltpu.VMEM((15, 32, 256), F32),
            pltpu.VMEM((32, 256), F32),
            dma((2,)), dma((2,)), dma((2,)), dma((2,)), dma((2,)), dma((2,)), dma, dma((4,)), dma((4, 2)),
        ],
        compiler_params=pltpu.CompilerParams(
            vmem_limit_bytes=VMEM_CAP, collective_id=0, has_side_effects=True
        ),
    )(sums, late, feat)


def passed_along(block, axis, distance):
    devices = range(lax.axis_size(axis))
    route = [(i - distance, i) for i in devices if i - distance in devices]
    return lax.ppermute(block, axis, route)


def local(volume, kernel_one, kernel_two, cotangent):
    shape = jax.ShapeDtypeStruct
    spread, taps = spread_matrix(), tap_matrix()
    rim = passed_along(volume[:, :, 1:], "space", 1)
    sums, feat, g2, uu, slope = pl.pallas_call(
        forward_kernel,
        name="forward",
        out_shape=(
            shape((1024, 512), BF16), shape((512, 128), F32), shape((64, 1024), BF16),
            shape((640, 1024), BF16), shape((256, 1024), F32),
        ),
        in_specs=[VM] * 7,
        out_specs=(VM,) * 5,
        scratch_shapes=[
            pltpu.VMEM((28, 136, 128), F32),
            pltpu.VMEM((1120, 512), F32),
            pltpu.VMEM((7 * 1024, 128), F32),
            pltpu.VMEM((896, 1024), BF16),
            pltpu.VMEM((32, 128), BF16),
            pltpu.VMEM((128, 384), BF16),
            pltpu.VMEM((8, 864, 128), F32),
            pltpu.VMEM((1280, 1024), BF16),
            pltpu.VMEM((32, 512), F32),
        ],
        compiler_params=pltpu.CompilerParams(vmem_limit_bytes=VMEM_CAP),
    )(volume, rim, kernel_one.T, kernel_two.T, cotangent.reshape(64, 1024), spread, taps)
    above = passed_along(g2, "space", -1)
    late = pl.pallas_call(
        backward_kernel,
        name="backward",
        out_shape=shape((32, 256), F32),
        in_specs=[VM] * 6,
        out_specs=VM,
        scratch_shapes=[
            pltpu.VMEM((864, 128), F32),
            pltpu.VMEM((3, 128, 256), BF16),
            pltpu.VMEM((2, 256, 1024), BF16),
        ],
        compiler_params=pltpu.CompilerParams(vmem_limit_bytes=VMEM_CAP),
    )(uu, slope, g2, above, kernel_two.T, taps)
    sums, late, feat = summed(sums, late, feat)
    features, in_one, in_two, out_one, out_two, w_one, w_two = pl.pallas_call(
        unpack_kernel,
        name="unpack",
        out_shape=(
            shape((64, 1, 16, 64), BF16), shape((108, 108), F32), shape((864, 864), F32), shape((32, 32), F32),
            shape((64, 64), F32), shape((32, 108), F32), shape((64, 864), F32),
        ),
        in_specs=[VM] * 3,
        out_specs=(VM,) * 7,
        compiler_params=pltpu.CompilerParams(vmem_limit_bytes=VMEM_CAP),
    )(sums, late, feat)
    return features.transpose(0, 1, 3, 2), in_one, in_two, out_one, out_two, w_one.T, w_two.T


def solution(mesh):
    placed = (P(None, "batch", "space", None, None), P(), P(), P(None, "batch", "space", None))
    return jax.shard_map(
        local,
        mesh=mesh,
        in_specs=placed,
        out_specs=(P(None, "batch", None, "space"), P(), P(), P(), P(), P(), P()),
        check_vma=False,
    )
```

```python
import math

import jax
import jax.numpy as jnp
import numpy as np
from jax import lax
from jax.experimental import pallas as pl
from jax.experimental.pallas import tpu as pltpu
from jax.sharding import PartitionSpec as P

F32 = jnp.float32
BF16 = jnp.bfloat16
VMEM_CAP = 56 * 1024 * 1024
TOTAL_ONE = 2 * 128 * 64 * 64
TOTAL_TWO = 2 * 64 * 32 * 32


def tap_matrix():
    table = np.zeros((128, 4, 3, 128), np.float32)
    for p in range(2):
        for q in range(2):
            for c in range(4):
                for a in range(3):
                    for b in range(3):
                        for e in range(3):
                            row = c * 27 + a * 9 + b * 3 + e
                            table[row, p * 2 + q, a, (2 * q + e) * 20 + c * 5 + 2 * p + b] = 1
    return jnp.asarray(table.reshape(128, 1536), F32)


def gelu_parts(value):
    square = value * value
    tangent = jnp.tanh(0.7978845608028654 * (value + 0.044715 * value * square))
    half = 0.5 * (1.0 + tangent)
    slope = half + 0.5 * value * (1.0 - tangent * tangent) * 0.7978845608028654 * (1.0 + 3.0 * 0.044715 * square)
    return value * half, slope


def dot(a, b):
    return lax.dot_general(a, b, (((1,), (0,)), ((), ())), preferred_element_type=F32)


def dot_nt(a, b):
    return lax.dot_general(a, b, (((1,), (1,)), ((), ())), preferred_element_type=F32)


def halves(value):
    high = value.astype(BF16)
    return high, (value - high.astype(F32)).astype(BF16)


VM = pl.BlockSpec(memory_space=pltpu.VMEM)
MESH = pl.DeviceIdType.MESH


def shifted(me, k):
    y = lax.rem(me // 16 + k // 16, 4)
    z = lax.rem(lax.rem(me // 4, 4) + lax.rem(k // 4, 4), 4)
    x = lax.rem(lax.rem(me, 4) + lax.rem(k, 4), 4)
    return y * 16 + z * 4 + x


def rows(index, count=16):
    return pl.ds(pl.multiple_of(index * count, count), count)


def await_bytes(ref, sem):
    pltpu.make_async_copy(ref, ref, sem).wait()


def spread_planes(first, count, load, vf, lf, of, uu, ee):
    def split(zz, carry):
        for c in range(4):
            at = zz * 4 + c
            vf[at, 8:136, :] = load(c, zz)
            for res in range(5):
                row = pl.ds(pl.multiple_of(at * 40 + res * 8, 8), 8)
                for m in range(4):
                    lf[row, m * 128 : (m + 1) * 128] = vf[at, pl.ds(7 + 4 * m + res, 8, stride=16), :]
        return carry

    lax.fori_loop(0, count, split, 0)
    parts = dot(lf[0 : count * 160, :].astype(BF16), ee[...])
    for zz in range(count):
        for res in range(5):
            of[zz * 1024 + res * 160 : zz * 1024 + (res + 1) * 160, :] = parts[
                zz * 160 : (zz + 1) * 160, res * 128 : (res + 1) * 128
            ]

    def flatten(zz, carry):
        for group in range(7):
            for j in range(8):
                start = zz * 1024 + group * 128 + j
                part = jnp.concatenate(
                    [of[pl.ds(start, 8, stride=8), :], of[pl.ds(start + 64, 8, stride=8), :]], axis=0
                )
                at = pl.ds(pl.multiple_of((first + zz) * 128 + group * 16, 16), 16)
                uu[at, j * 128 : (j + 1) * 128] = part.astype(BF16)
        uu[pl.ds(pl.multiple_of((first + zz) * 128 + 112, 16), 16), :] = jnp.zeros((16, 1024), BF16)
        return carry

    lax.fori_loop(0, count, flatten, 0)


def place_taps(act, a, p2f):
    lane = lax.broadcasted_iota(jnp.int32, (1, 1024), 1)
    for b in range(3):
        for e in range(3):
            p, q = (b + 1) % 2, (e + 1) % 2
            block = act[(p * 2 + q) * 32 : (p * 2 + q + 1) * 32, :]
            if e == 0:
                block = jnp.where(lane % 32 == 0, 0.0, pltpu.roll(block, 1, 1))
            if b == 0:
                block = jnp.where(lane < 32, 0.0, pltpu.roll(block, 32, 1))
            for j in range(8):
                p2f[j, pl.ds(a * 9 + b * 3 + e, 32, stride=27), :] = block[:, j * 128 : (j + 1) * 128]


def first_factor(uu, taps, tiles):
    gram = dot_nt(uu[0:384, :], uu[0:384, :]) + dot_nt(uu[256:640, :], uu[256:640, :])
    total = jnp.zeros((128, 128), F32)
    for part in halves(gram):
        for pq in range(4):
            tap = taps[:, pq * 384 : (pq + 1) * 384]
            total = total + dot(tap, dot_nt(part, tap).astype(BF16))
    total = total * (1.0 / TOTAL_ONE)
    for k in range(4):
        tiles[:, k * 128 : (k + 1) * 128] = total[k * 32 : (k + 1) * 32, :]


def swap_groups(act):
    chan = lax.broadcasted_iota(jnp.int32, (64, 1024), 0) % 8
    group = (lax.broadcasted_iota(jnp.int32, (64, 1024), 1) // 16) % 8
    for bit in (4, 2, 1):
        down = pltpu.roll(pltpu.roll(act, 64 - bit, 0), bit * 16, 1)
        up = pltpu.roll(pltpu.roll(act, bit, 0), 1024 - bit * 16, 1)
        in_chan = (chan & bit) != 0
        in_group = (group & bit) != 0
        act = jnp.where(in_chan == in_group, act, jnp.where(in_group, down, up))
    return act


def backward_weights(k2_ref, k2f, aa):
    k2f[:, 0:64] = k2_ref[...].astype(F32).T
    aa[...] = jnp.zeros((3, 128, 256), BF16)
    for a in range(3):
        for b in range(3):
            for e in range(3):
                p, q = (b + 1) % 2, (e + 1) % 2
                sy, sx = int(b == 0), int(e == 0)
                block = k2f[pl.ds(a * 9 + b * 3 + e, 32, stride=27), :]
                at = (p * 2 + q) * 32
                aa[a, at : at + 32, (sy * 2 + sx) * 64 : (sy * 2 + sx + 1) * 64] = block[:, 0:64].astype(BF16)


def shift_back(value, gs, n):
    lane = lax.broadcasted_iota(jnp.int32, (1, 1024), 1)
    for sy in range(2):
        for sx in range(2):
            moved = value
            if sx:
                moved = jnp.where(lane % 32 == 31, 0.0, pltpu.roll(moved, 1023, 1))
            if sy:
                moved = jnp.where(lane >= 992, 0.0, pltpu.roll(moved, 992, 1))
            gs[n, (sy * 2 + sx) * 64 : (sy * 2 + sx + 1) * 64, :] = moved.astype(BF16)


def step_kernel(
    vol_ref, k1_ref, k2_ref, cot_ref, tap_ref, out_ref, late_out_ref, feat_out_ref,
    vf, lf, of, uu, ee, taps, k1p, ww, slopes, hid, p2f, p2b, tiles, sums, feat, g2, k2f, aa, gs,
    rim, hid_in, g2_in, pair, half, got, late, late_pair, late_x, late_sum, late_yz, late_total,
    rim_sem, hid_sem, g2_sem, pair_sem, late_pair_sem, rs_sem, feat_sem, x_sem, yz_sem,
    gather_send, gather_recv, back_sem,
):
    me, core = lax.axis_index("space"), lax.axis_index("batch")
    sibling = (me, 1 - core)
    above, below = (lax.rem(me + 1, 64), core), (lax.rem(me + 63, 64), core)
    mine = pl.ds(pl.multiple_of(core * 256, 256), 256)
    other = pl.ds(pl.multiple_of((1 - core) * 256, 256), 256)

    def send(src, dst, sems, to):
        copy = pltpu.make_async_remote_copy(
            src_ref=src, dst_ref=dst, send_sem=sems.at[0], recv_sem=sems.at[1], device_id=to, device_id_type=MESH
        )
        copy.start()
        return copy

    barrier = pltpu.get_barrier_semaphore()
    pl.semaphore_signal(barrier, inc=1, device_id=sibling, device_id_type=MESH)

    def greet(k, carry):
        pl.semaphore_signal(barrier, inc=1, device_id=(shifted(me, k), core), device_id_type=MESH)
        return carry

    lax.fori_loop(1, 64, greet, 0)

    at_x = lax.broadcasted_iota(jnp.int32, (128, 128), 0)
    lane = lax.broadcasted_iota(jnp.int32, (128, 128), 1)
    for m in range(4):
        for res in range(5):
            hit = (at_x == 4 * (lane - 32 * m) + (res - 1)) & (lane >= 32 * m) & (lane < 32 * (m + 1))
            ee[m * 128 : (m + 1) * 128, res * 128 : (res + 1) * 128] = jnp.where(hit, 1.0, 0.0).astype(BF16)
    vf[:, 0:8, :] = jnp.zeros((16, 8, 128), F32)
    for zz in range(4):
        of[zz * 1024 + 800 : zz * 1024 + 896, :] = jnp.zeros((96, 128), F32)
    taps[...] = tap_ref[...].astype(BF16)
    k1p[...] = jnp.zeros((32, 128), BF16)
    k1p[:, 0:108] = k1_ref[...]
    wide = dot(k1p[...], taps[...])
    for pq in range(4):
        ww[pq * 32 : (pq + 1) * 32, :] = wide[:, pq * 384 : (pq + 1) * 384].astype(BF16)

    spread_planes(1, 4, lambda c, zz: vol_ref[c, 0, zz].astype(F32), vf, lf, of, uu, ee)
    pl.semaphore_wait(barrier, 64)
    rim_copy = send(vol_ref.at[:, 0, 3], rim, rim_sem, above)
    act, slope = gelu_parts(dot(ww[...], uu[256:640, :]))
    slopes[128:256, :] = slope
    hid[...] = act.astype(BF16)
    hid_copy = send(hid, hid_in, hid_sem, above)
    place_taps(hid[...].astype(F32), 2, p2f)
    backward_weights(k2_ref, k2f, aa)

    rim_copy.wait()
    spread_planes(
        0, 1, lambda c, zz: jnp.where(me > 0, rim[c].astype(F32), 0.0), vf, lf, of, uu, ee
    )
    act, slope = gelu_parts(dot(ww[...], uu[0:384, :]))
    slopes[0:128, :] = slope
    place_taps(act.astype(BF16).astype(F32), 1, p2f)
    first_factor(uu, taps, tiles)

    hid_copy.wait()
    place_taps(jnp.where(me > 0, hid_in[...].astype(F32), 0.0), 0, p2f)
    for j in range(8):
        p2b[0:864, j * 128 : (j + 1) * 128] = p2f[j].astype(BF16)
    p2b[864:896, :] = jnp.zeros((32, 1024), BF16)
    p2b[896:1280, :] = p2b[0:384, :]
    act, slope = gelu_parts(dot(k2_ref[...], p2b[0:864, :]))
    g2[...] = (cot_ref[...].astype(F32) * (1.0 / math.sqrt(TOTAL_TWO)) * slope).astype(BF16)
    g2_copy = send(g2, g2_in, g2_sem, below)
    pre_act = act.astype(BF16).astype(F32)

    pairs = []

    def swap_block(i):
        block = slice(i * 128, (i + 1) * 128)
        pairs.append(send(sums.at[block, other], pair.at[block, :], pair_sem.at[i], sibling))

    grads = dot_nt(g2[...], p2b[0:896, :])
    own = dot_nt(g2[...], g2[...])
    sums[896:960, :] = grads[:, 0:512].astype(BF16)
    sums[960:1024, 0:384] = grads[:, 512:896].astype(BF16)
    sums[960:1024, 384:512] = jnp.concatenate([own, jnp.zeros((64, 64), F32)], axis=1).astype(BF16)
    swap_block(7)
    for i in (6, 0, 1, 2, 3, 4, 5):
        block = dot_nt(p2b[i * 128 : (i + 1) * 128, :], p2b[i * 128 : i * 128 + 512, :]) * (1.0 / TOTAL_TWO)
        sums[i * 128 : (i + 1) * 128, :] = block.astype(BF16)
        if i == 6:
            sums[864:896, :] = tiles[...].astype(BF16)
        swap_block(i)
    for n, i in enumerate((7, 6, 0, 1, 2, 3, 4, 5)):
        block = slice(i * 128, (i + 1) * 128)
        pairs[n].wait()
        half[block, :] = (sums[block, mine].astype(F32) + pair[block, :].astype(F32)).astype(BF16)

    def scatter(k, carry):
        to = shifted(me, k)
        send(half.at[rows(to), :], got.at[rows(k - 1), :], rs_sem, (to, core))
        return carry

    lax.fori_loop(1, 64, scatter, 0)

    moved = swap_groups(pre_act)
    for r in range(8):
        for g in range(8):
            feat[pl.ds(64 * g + r, 8, stride=8), :] = moved[r * 8 : (r + 1) * 8, g * 128 : (g + 1) * 128]

    def hand_on(k, carry):
        to = shifted(me, k)
        send(feat.at[rows(to, 8), :], feat_out_ref.at[rows(me, 8), :], feat_sem, (to, core))
        return carry

    lax.fori_loop(1, 64, hand_on, 0)
    feat_out_ref[rows(me, 8), :] = feat[rows(me, 8), :]

    shift_back(g2[...].astype(F32), gs, 0)
    g2_copy.wait()
    shift_back(jnp.where(me < 63, g2_in[...].astype(F32), 0.0), gs, 1)
    cross = jnp.zeros((128, 384), F32)
    gram = jnp.zeros((128, 128), F32)
    for h in range(2):
        spread = dot(aa[h + 1], gs[0])
        if h == 1:
            spread = spread + dot(aa[0], gs[1])
        g1 = (spread * slopes[h * 128 : (h + 1) * 128, :]).astype(BF16)
        cross = cross + dot_nt(g1, uu[h * 256 : h * 256 + 384, :])
        gram = gram + dot_nt(g1, g1)
    weight = jnp.zeros((32, 128), F32)
    own = jnp.zeros((32, 32), F32)
    for pq in range(4):
        for part in halves(cross[pq * 32 : (pq + 1) * 32, :]):
            weight = weight + dot_nt(part, taps[:, pq * 384 : (pq + 1) * 384])
        own = own + gram[pq * 32 : (pq + 1) * 32, pq * 32 : (pq + 1) * 32]
    late[:, 0:128] = weight
    late[:, 128:256] = jnp.concatenate([own, jnp.zeros((32, 96), F32)], axis=1)
    late_copy = send(late, late_pair, late_pair_sem, sibling)

    await_bytes(got, rs_sem.at[1])

    def add(k, total):
        return total + got[rows(k), :].astype(F32)

    total = lax.fori_loop(0, 63, add, half[rows(me), :].astype(F32), unroll=9)
    out_ref[rows(me), mine] = total.astype(BF16)

    def gather(k, carry):
        piece = out_ref.at[rows(me), mine]
        copy = pltpu.make_async_remote_copy(
            src_ref=piece, dst_ref=piece, send_sem=gather_send, recv_sem=gather_recv.at[k // 16],
            device_id=(shifted(me, k), core), device_id_type=MESH,
        )
        copy.start()
        return carry

    lax.fori_loop(1, 64, gather, 0)

    late_copy.wait()
    late_sum[...] = late[...] + late_pair[...]

    def along_x(k, carry):
        send(late_sum, late_x.at[k - 1], x_sem, (shifted(me, k), core))
        return carry

    lax.fori_loop(1, 4, along_x, 0)
    await_bytes(late_x, x_sem.at[0])
    await_bytes(late_x, x_sem.at[1])
    late_total[...] = late_sum[...] + (late_x[0] + late_x[1] + late_x[2])

    def across(k, carry):
        send(late_total, late_yz.at[k - 1], yz_sem, (shifted(me, 4 * k), core))
        return carry

    lax.fori_loop(1, 16, across, 0)

    backs = []
    for k in range(4):
        count = 240 if k == 0 else 256
        await_bytes(half.at[0:count, :], gather_recv.at[k])
        block = pl.ds(pl.multiple_of(lax.rem(me // 16 + 4 - k, 4) * 256, 256), 256)
        backs.append(send(out_ref.at[block, mine], out_ref.at[block, mine], back_sem.at[k], sibling))
    await_bytes(late_yz, yz_sem.at[0])
    await_bytes(late_yz, yz_sem.at[1])
    late_out_ref[...] = lax.fori_loop(0, 15, lambda k, total: total + late_yz[k], late_total[...], unroll=5)
    await_bytes(got, rs_sem.at[0])
    await_bytes(got, gather_send)
    for sem in (feat_sem.at[0], feat_sem.at[1]):
        await_bytes(feat_out_ref.at[0:504, :], sem)
    for copy in backs:
        copy.wait()


def unpack_kernel(
    sums_ref, late_ref, feat_ref,
    features_ref, in_one_ref, in_two_ref, out_one_ref, out_two_ref, w_one_ref, w_two_ref,
):
    for i in range(7):
        rows = min(128, 864 - i * 128)
        for k in range(4):
            j = (i + k) % 7
            cols = min(128, 864 - j * 128)
            block = sums_ref[i * 128 : (i + 1) * 128, k * 128 : (k + 1) * 128].astype(F32)
            in_two_ref[i * 128 : i * 128 + rows, j * 128 : j * 128 + cols] = block[0:rows, 0:cols]
            if k:
                in_two_ref[j * 128 : j * 128 + cols, i * 128 : i * 128 + rows] = block.T[0:cols, 0:rows]
    w_two_ref[:, 0:512] = sums_ref[896:960, :].astype(F32)
    rest = sums_ref[960:1024, :].astype(F32)
    w_two_ref[:, 512:864] = rest[:, 0:352]
    out_two_ref[...] = rest[:, 384:448]
    first = sums_ref[864:896, :].astype(F32)
    for k in range(4):
        rows = min(32, 108 - k * 32)
        in_one_ref[k * 32 : k * 32 + rows, :] = first[0:rows, k * 128 : k * 128 + 108]
    late = late_ref[...]
    w_one_ref[...] = late[:, 0:108]
    out_one_ref[...] = late[:, 128:160]
    for r in range(8):
        block = feat_ref[pl.ds(r, 64, stride=8), :]
        features_ref[r * 8 : (r + 1) * 8, 0, :, :] = block.T.reshape(8, 16, 64).astype(BF16)


def local(volume, kernel_one, kernel_two, cotangent):
    shape = jax.ShapeDtypeStruct
    dma = pltpu.SemaphoreType.DMA
    buf = pltpu.VMEM
    sums, late, feat = pl.pallas_call(
        step_kernel,
        name="step",
        out_shape=(shape((1024, 512), BF16), shape((32, 256), F32), shape((512, 128), F32)),
        in_specs=[VM] * 5,
        out_specs=(VM,) * 3,
        scratch_shapes=[
            buf((16, 136, 128), F32), buf((640, 512), F32), buf((4096, 128), F32), buf((640, 1024), BF16),
            buf((512, 640), BF16), buf((128, 1536), BF16), buf((32, 128), BF16), buf((128, 384), BF16),
            buf((256, 1024), F32), buf((128, 1024), BF16), buf((8, 864, 128), F32), buf((1280, 1024), BF16),
            buf((32, 512), F32), buf((1024, 512), BF16), buf((512, 128), F32), buf((64, 1024), BF16),
            buf((864, 128), F32), buf((3, 128, 256), BF16), buf((2, 256, 1024), BF16),
            buf((4, 128, 128), BF16), buf((128, 1024), BF16), buf((64, 1024), BF16),
            buf((1024, 256), BF16), buf((1024, 256), BF16), buf((1008, 256), BF16),
            buf((32, 256), F32), buf((32, 256), F32), buf((3, 32, 256), F32), buf((32, 256), F32),
            buf((15, 32, 256), F32), buf((32, 256), F32),
            dma((2,)), dma((2,)), dma((2,)), dma((8, 2)), dma((2,)), dma((2,)), dma((2,)), dma((2,)), dma((2,)),
            dma, dma((4,)), dma((4, 2)),
        ],
        compiler_params=pltpu.CompilerParams(
            vmem_limit_bytes=VMEM_CAP, collective_id=0, has_side_effects=True
        ),
    )(volume, kernel_one.T, kernel_two.T, cotangent.reshape(64, 1024), tap_matrix())
    features, in_one, in_two, out_one, out_two, w_one, w_two = pl.pallas_call(
        unpack_kernel,
        name="unpack",
        out_shape=(
            shape((64, 1, 16, 64), BF16), shape((108, 108), F32), shape((864, 864), F32), shape((32, 32), F32),
            shape((64, 64), F32), shape((32, 108), F32), shape((64, 864), F32),
        ),
        in_specs=[VM] * 3,
        out_specs=(VM,) * 7,
        compiler_params=pltpu.CompilerParams(vmem_limit_bytes=VMEM_CAP),
    )(sums, late, feat)
    return features.transpose(0, 1, 3, 2), in_one, in_two, out_one, out_two, w_one.T, w_two.T


def solution(mesh):
    placed = (P(None, "batch", "space", None, None), P(), P(), P(None, "batch", "space", None))
    return jax.shard_map(
        local,
        mesh=mesh,
        in_specs=placed,
        out_specs=(P(None, "batch", None, "space"), P(), P(), P(), P(), P(), P()),
        check_vma=False,
    )
```

```python
import math

import jax
import jax.numpy as jnp
import numpy as np
from jax import lax
from jax.experimental import pallas as pl
from jax.experimental.pallas import tpu as pltpu
from jax.sharding import PartitionSpec as P

F32 = jnp.float32
BF16 = jnp.bfloat16
VMEM_CAP = 56 * 1024 * 1024
TOTAL_ONE = 2 * 128 * 64 * 64
TOTAL_TWO = 2 * 64 * 32 * 32


def tap_matrix():
    table = np.zeros((128, 3, 128), np.float32)
    for c in range(4):
        for a in range(3):
            for b in range(3):
                for e in range(3):
                    table[c * 27 + a * 9 + b * 3 + e, a, e * 20 + c * 5 + b] = 1
    return jnp.asarray(table.reshape(128, 384), F32)


def gelu_parts(value):
    square = value * value
    tangent = jnp.tanh(0.7978845608028654 * (value + 0.044715 * value * square))
    half = 0.5 * (1.0 + tangent)
    slope = half + 0.5 * value * (1.0 - tangent * tangent) * 0.7978845608028654 * (1.0 + 3.0 * 0.044715 * square)
    return value * half, slope


def dot(a, b):
    return lax.dot_general(a, b, (((1,), (0,)), ((), ())), preferred_element_type=F32)


def dot_nt(a, b):
    return lax.dot_general(a, b, (((1,), (1,)), ((), ())), preferred_element_type=F32)


def halves(value):
    high = value.astype(BF16)
    return high, (value - high.astype(F32)).astype(BF16)


VM = pl.BlockSpec(memory_space=pltpu.VMEM)
MESH = pl.DeviceIdType.MESH


def shifted(me, k):
    return (((me & 48) + (k & 48)) & 48) | (((me & 12) + (k & 12)) & 12) | (((me & 3) + (k & 3)) & 3)


def rows(index, count=16):
    return pl.ds(pl.multiple_of(index * count, count), count)


def await_bytes(ref, sem):
    pltpu.make_async_copy(ref, ref, sem).wait()


def spread_planes(first, count, load, vf, lf, of, uu, ee):
    def split(zz, carry):
        for c in range(4):
            at = zz * 4 + c
            vf[at, 8:136, :] = load(c, zz)
            for res in range(5):
                row = pl.ds(pl.multiple_of(at * 40 + res * 8, 8), 8)
                for m in range(4):
                    lf[row, m * 128 : (m + 1) * 128] = vf[at, pl.ds(7 + 4 * m + res, 8, stride=16), :]
        return carry

    lax.fori_loop(0, count, split, 0)
    parts = dot(lf[0 : count * 160, :].astype(BF16), ee[...])
    for zz in range(count):
        for res in range(5):
            of[zz * 1024 + res * 160 : zz * 1024 + (res + 1) * 160, :] = parts[
                zz * 160 : (zz + 1) * 160, res * 128 : (res + 1) * 128
            ]

    def flatten(zz, carry):
        for group in range(7):
            for j in range(8):
                start = zz * 1024 + group * 128 + j
                part = jnp.concatenate(
                    [of[pl.ds(start, 8, stride=8), :], of[pl.ds(start + 64, 8, stride=8), :]], axis=0
                )
                at = pl.ds(pl.multiple_of((first + zz) * 128 + group * 16, 16), 16)
                uu[at, j * 128 : (j + 1) * 128] = part.astype(BF16)
        uu[pl.ds(pl.multiple_of((first + zz) * 128 + 112, 16), 16), :] = jnp.zeros((16, 1024), BF16)
        return carry

    lax.fori_loop(0, count, flatten, 0)


def place_taps(act, a, p2f):
    lane = lax.broadcasted_iota(jnp.int32, (1, 1024), 1)
    for b in range(3):
        for e in range(3):
            p, q = (b + 1) % 2, (e + 1) % 2
            block = act[(p * 2 + q) * 32 : (p * 2 + q + 1) * 32, :]
            if e == 0:
                block = jnp.where(lane % 32 == 0, 0.0, pltpu.roll(block, 1, 1))
            if b == 0:
                block = jnp.where(lane < 32, 0.0, pltpu.roll(block, 32, 1))
            for j in range(8):
                p2f[j, pl.ds(a * 9 + b * 3 + e, 32, stride=27), :] = block[:, j * 128 : (j + 1) * 128]


def first_factor(uu, taps, tiles):
    gram = dot_nt(uu[0:384, :], uu[0:384, :]) + dot_nt(uu[256:640, :], uu[256:640, :])
    total = jnp.zeros((128, 128), F32)
    for part in halves(gram):
        for pq in range(4):
            tap = taps[:, pq * 384 : (pq + 1) * 384]
            total = total + dot(tap, dot_nt(part, tap).astype(BF16))
    total = total * (1.0 / TOTAL_ONE)
    for k in range(4):
        tiles[:, k * 128 : (k + 1) * 128] = total[k * 32 : (k + 1) * 32, :]


def swap_groups(act):
    chan = lax.broadcasted_iota(jnp.int32, (64, 1024), 0) % 8
    group = (lax.broadcasted_iota(jnp.int32, (64, 1024), 1) // 16) % 8
    for bit in (4, 2, 1):
        down = pltpu.roll(pltpu.roll(act, 64 - bit, 0), bit * 16, 1)
        up = pltpu.roll(pltpu.roll(act, bit, 0), 1024 - bit * 16, 1)
        in_chan = (chan & bit) != 0
        in_group = (group & bit) != 0
        act = jnp.where(in_chan == in_group, act, jnp.where(in_group, down, up))
    return act


def backward_weights(k2_ref, k2f, aa):
    k2f[:, 0:64] = k2_ref[...].astype(F32).T
    aa[...] = jnp.zeros((3, 128, 256), BF16)
    for a in range(3):
        for b in range(3):
            for e in range(3):
                p, q = (b + 1) % 2, (e + 1) % 2
                sy, sx = int(b == 0), int(e == 0)
                block = k2f[pl.ds(a * 9 + b * 3 + e, 32, stride=27), :]
                at = (p * 2 + q) * 32
                aa[a, at : at + 32, (sy * 2 + sx) * 64 : (sy * 2 + sx + 1) * 64] = block[:, 0:64].astype(BF16)


def shift_back(value, gs, n):
    lane = lax.broadcasted_iota(jnp.int32, (1, 1024), 1)
    for sy in range(2):
        for sx in range(2):
            moved = value
            if sx:
                moved = jnp.where(lane % 32 == 31, 0.0, pltpu.roll(moved, 1023, 1))
            if sy:
                moved = jnp.where(lane >= 992, 0.0, pltpu.roll(moved, 992, 1))
            gs[n, (sy * 2 + sx) * 64 : (sy * 2 + sx + 1) * 64, :] = moved.astype(BF16)


def step_kernel(
    vol_hbm, k1_hbm, k2_hbm, cot_hbm, tap_hbm, out_ref, late_out_ref, feat_out_ref,
    vol_ref, k1_ref, k2_ref, cot_ref, tap_ref, load_sem, vf, lf, of, uu, ee, taps, k1p, ww, slopes, hid, p2f, p2b, tiles, sums, feat, g2, k2f, aa, gs,
    rim, hid_in, g2_in, pair, half, got, late, late_pair, late_x, late_sum, late_yz, late_total,
    rim_sem, hid_sem, g2_sem, pair_sem, late_pair_sem, rs_sem, feat_sem, x_sem, yz_sem,
    gather_send, gather_recv, back_sem, late_back_sem,
):
    me, core = lax.axis_index("space"), lax.axis_index("batch")
    sibling = (me, 1 - core)
    above, below = (lax.rem(me + 1, 64), core), (lax.rem(me + 63, 64), core)
    mine = pl.ds(pl.multiple_of(core * 256, 256), 256)
    other = pl.ds(pl.multiple_of((1 - core) * 256, 256), 256)

    def send(src, dst, sems, to):
        copy = pltpu.make_async_remote_copy(
            src_ref=src, dst_ref=dst, send_sem=sems.at[0], recv_sem=sems.at[1], device_id=to, device_id_type=MESH
        )
        copy.start()
        return copy

    barrier = pltpu.get_barrier_semaphore()
    pl.semaphore_signal(barrier, inc=1, device_id=sibling, device_id_type=MESH)

    for k in range(1, 64):
        pl.semaphore_signal(barrier, inc=1, device_id=(shifted(me, k), core), device_id_type=MESH)
    loads = [
        pltpu.make_async_copy(src, dst, load_sem.at[n])
        for n, (src, dst) in enumerate(
            ((vol_hbm, vol_ref), (tap_hbm, tap_ref), (k1_hbm, k1_ref), (k2_hbm, k2_ref), (cot_hbm, cot_ref))
        )
    ]
    for load in loads:
        load.start()

    at_x = lax.broadcasted_iota(jnp.int32, (128, 128), 0)
    lane = lax.broadcasted_iota(jnp.int32, (128, 128), 1)
    for m in range(4):
        for res in range(5):
            hit = (at_x == 4 * (lane - 32 * m) + (res - 1)) & (lane >= 32 * m) & (lane < 32 * (m + 1))
            ee[m * 128 : (m + 1) * 128, res * 128 : (res + 1) * 128] = jnp.where(hit, 1.0, 0.0).astype(BF16)
    vf[:, 0:8, :] = jnp.zeros((16, 8, 128), F32)
    for zz in range(4):
        of[zz * 1024 + 800 : zz * 1024 + 896, :] = jnp.zeros((96, 128), F32)
    for load in loads:
        load.wait()
    for pq, step in enumerate((0, 40, 2, 42)):
        moved = tap_ref[...] if step == 0 else pltpu.roll(tap_ref[...], step, 1)
        taps[:, pq * 384 : (pq + 1) * 384] = moved.astype(BF16)
    k1p[...] = jnp.zeros((32, 128), BF16)
    k1p[:, 0:108] = k1_ref[...]
    wide = dot(k1p[...], taps[...])
    for pq in range(4):
        ww[pq * 32 : (pq + 1) * 32, :] = wide[:, pq * 384 : (pq + 1) * 384].astype(BF16)

    spread_planes(1, 4, lambda c, zz: vol_ref[c, 0, zz].astype(F32), vf, lf, of, uu, ee)
    pl.semaphore_wait(barrier, 64)
    rim_copy = send(vol_ref.at[:, 0, 3], rim, rim_sem, above)
    act, slope = gelu_parts(dot(ww[...], uu[256:640, :]))
    slopes[128:256, :] = slope
    hid[...] = act.astype(BF16)
    hid_copy = send(hid, hid_in, hid_sem, above)
    place_taps(hid[...].astype(F32), 2, p2f)
    backward_weights(k2_ref, k2f, aa)

    rim_copy.wait()
    spread_planes(
        0, 1, lambda c, zz: jnp.where(me > 0, rim[c].astype(F32), 0.0), vf, lf, of, uu, ee
    )
    act, slope = gelu_parts(dot(ww[...], uu[0:384, :]))
    slopes[0:128, :] = slope
    place_taps(act.astype(BF16).astype(F32), 1, p2f)
    first_factor(uu, taps, tiles)

    hid_copy.wait()
    place_taps(jnp.where(me > 0, hid_in[...].astype(F32), 0.0), 0, p2f)
    for j in range(8):
        p2b[0:864, j * 128 : (j + 1) * 128] = p2f[j].astype(BF16)
    p2b[864:896, :] = jnp.zeros((32, 1024), BF16)
    p2b[896:1280, :] = p2b[0:384, :]

    pairs = {}

    def swap_block(i):
        block = slice(i * 128, (i + 1) * 128)
        pairs[i] = send(sums.at[block, other], pair.at[block, :], pair_sem.at[i], sibling)

    def add_block(i):
        block = slice(i * 128, (i + 1) * 128)
        pairs[i].wait()
        half[block, :] = (sums[block, mine].astype(F32) + pair[block, :].astype(F32)).astype(BF16)

    def scatter(k):
        to = shifted(me, k)
        send(half.at[rows(to), :], got.at[rows(k - 1), :], rs_sem, (to, core))

    for i in (6, 0, 1, 2, 3, 4, 5):
        block = dot_nt(p2b[i * 128 : (i + 1) * 128, :], p2b[i * 128 : i * 128 + 512, :]) * (1.0 / TOTAL_TWO)
        sums[i * 128 : (i + 1) * 128, :] = block.astype(BF16)
        if i == 6:
            sums[864:896, :] = tiles[...].astype(BF16)
        swap_block(i)
    act, slope = gelu_parts(dot(k2_ref[...], p2b[0:864, :]))
    g2[...] = (cot_ref[...].astype(F32) * (1.0 / math.sqrt(TOTAL_TWO)) * slope).astype(BF16)
    g2_copy = send(g2, g2_in, g2_sem, below)
    pre_act = act.astype(BF16).astype(F32)
    for i in (6, 0, 1, 2, 3, 4, 5):
        add_block(i)

    @pl.loop(1, 64)
    def _(k):
        @pl.when(shifted(me, k) < 56)
        def _():
            scatter(k)

    grads = dot_nt(g2[...], p2b[0:896, :])
    own = dot_nt(g2[...], g2[...])
    sums[896:960, :] = grads[:, 0:512].astype(BF16)
    sums[960:1024, 0:384] = grads[:, 512:896].astype(BF16)
    sums[960:1024, 384:512] = jnp.concatenate([own, jnp.zeros((64, 64), F32)], axis=1).astype(BF16)
    swap_block(7)
    shift_back(g2[...].astype(F32), gs, 0)
    add_block(7)

    @pl.loop(1, 64)
    def _(k):
        @pl.when(shifted(me, k) >= 56)
        def _():
            scatter(k)

    moved = swap_groups(pre_act)
    for r in range(8):
        for g in range(8):
            feat[pl.ds(64 * g + r, 8, stride=8), :] = moved[r * 8 : (r + 1) * 8, g * 128 : (g + 1) * 128]

    def hand_on(k, carry):
        to = shifted(me, k)
        send(feat.at[rows(to, 8), :], feat_out_ref.at[rows(me, 8), :], feat_sem, (to, core))
        return carry

    lax.fori_loop(1, 64, hand_on, 0)
    feat_out_ref[rows(me, 8), :] = feat[rows(me, 8), :]

    g2_copy.wait()
    shift_back(jnp.where(me < 63, g2_in[...].astype(F32), 0.0), gs, 1)
    cross = jnp.zeros((128, 384), F32)
    gram = jnp.zeros((128, 128), F32)
    for h in range(2):
        spread = dot(aa[h + 1], gs[0])
        if h == 1:
            spread = spread + dot(aa[0], gs[1])
        g1 = (spread * slopes[h * 128 : (h + 1) * 128, :]).astype(BF16)
        cross = cross + dot_nt(g1, uu[h * 256 : h * 256 + 384, :])
        gram = gram + dot_nt(g1, g1)
    weight = jnp.zeros((32, 128), F32)
    own = jnp.zeros((32, 32), F32)
    for pq in range(4):
        for part in halves(cross[pq * 32 : (pq + 1) * 32, :]):
            weight = weight + dot_nt(part, taps[:, pq * 384 : (pq + 1) * 384])
        own = own + gram[pq * 32 : (pq + 1) * 32, pq * 32 : (pq + 1) * 32]
    late[:, 0:128] = weight.astype(BF16)
    late[:, 128:256] = jnp.concatenate([own, jnp.zeros((32, 96), F32)], axis=1).astype(BF16)
    send(late.at[rows(1 - core), :], late_pair, late_pair_sem, sibling).wait()
    late_sum[...] = (late[rows(core), :].astype(F32) + late_pair[...].astype(F32)).astype(BF16)
    for k in range(1, 4):
        send(late_sum, late_x.at[k - 1], x_sem, (shifted(me, k), core))
    await_bytes(late_x, x_sem.at[0])
    await_bytes(late_x, x_sem.at[1])
    near = late_sum[...].astype(F32) + late_x[0].astype(F32) + (late_x[1].astype(F32) + late_x[2].astype(F32))
    late_total[...] = near.astype(BF16)
    for k in range(1, 16):
        send(late_total, late_yz.at[k - 1], yz_sem, (shifted(me, 4 * k), core))

    await_bytes(got, rs_sem.at[1])
    parts = [half[rows(me), :].astype(F32), jnp.zeros((16, 256), F32)]
    for k in range(63):
        parts[k % 2] = parts[k % 2] + got[k * 16 : (k + 1) * 16, :].astype(F32)
    out_ref[rows(me), mine] = (parts[0] + parts[1]).astype(BF16)

    def gather(k, carry):
        piece = out_ref.at[rows(me), mine]
        copy = pltpu.make_async_remote_copy(
            src_ref=piece, dst_ref=piece, send_sem=gather_send, recv_sem=gather_recv.at[k // 16],
            device_id=(shifted(me, k), core), device_id_type=MESH,
        )
        copy.start()
        return carry

    lax.fori_loop(1, 64, gather, 0)

    backs = []
    for k in range(4):
        count = 240 if k == 0 else 256
        await_bytes(half.at[0:count, :], gather_recv.at[k])
        block = pl.ds(pl.multiple_of(lax.rem(me // 16 + 4 - k, 4) * 256, 256), 256)
        backs.append(send(out_ref.at[block, mine], out_ref.at[block, mine], back_sem.at[k], sibling))
    await_bytes(late_yz, yz_sem.at[0])
    await_bytes(late_yz, yz_sem.at[1])
    far = late_total[...].astype(F32)
    for k in range(15):
        far = far + late_yz[k].astype(F32)
    late_out_ref[rows(core), :] = far
    backs.append(send(late_out_ref.at[rows(core), :], late_out_ref.at[rows(core), :], late_back_sem, sibling))
    await_bytes(got, rs_sem.at[0])
    await_bytes(got, gather_send)
    for sem in (feat_sem.at[0], feat_sem.at[1]):
        await_bytes(feat_out_ref.at[0:504, :], sem)
    for copy in backs:
        copy.wait()


def unpack_kernel(
    sums_ref, late_ref, feat_ref,
    features_ref, in_one_ref, in_two_hbm, out_one_ref, out_two_ref, w_one_ref, w_two_ref, in_two, store_sem,
):
    stores = []
    for i in range(7):
        height = min(128, 864 - i * 128)
        band = slice(i * 128, i * 128 + height)
        for k in range(-3, 4):
            j = (i + k) % 7
            width = min(128, 864 - j * 128)
            if k >= 0:
                block = sums_ref[i * 128 : (i + 1) * 128, k * 128 : (k + 1) * 128].astype(F32)
            else:
                block = sums_ref[j * 128 : (j + 1) * 128, -k * 128 : (1 - k) * 128].astype(F32).T
            in_two[band, j * 128 : j * 128 + width] = block[0:height, 0:width]
        stores.append(pltpu.make_async_copy(in_two.at[band, :], in_two_hbm.at[band, :], store_sem.at[i]))
        stores[-1].start()
    w_two_ref[:, 0:512] = sums_ref[896:960, :].astype(F32)
    rest = sums_ref[960:1024, :].astype(F32)
    w_two_ref[:, 512:864] = rest[:, 0:352]
    out_two_ref[...] = rest[:, 384:448]
    first = sums_ref[864:896, :].astype(F32)
    for k in range(4):
        height = min(32, 108 - k * 32)
        in_one_ref[k * 32 : k * 32 + height, :] = first[0:height, k * 128 : k * 128 + 108]
    late = late_ref[...]
    w_one_ref[...] = late[:, 0:108]
    out_one_ref[...] = late[:, 128:160]
    for r in range(8):
        block = feat_ref[pl.ds(r, 64, stride=8), :]
        features_ref[r * 8 : (r + 1) * 8, 0, :, :] = block.T.reshape(8, 16, 64).astype(BF16)
    for store in stores:
        store.wait()


def local(volume, kernel_one, kernel_two, cotangent):
    shape = jax.ShapeDtypeStruct
    dma = pltpu.SemaphoreType.DMA
    buf = pltpu.VMEM
    sums, late, feat = pl.pallas_call(
        step_kernel,
        name="step",
        out_shape=(shape((1024, 512), BF16), shape((32, 256), F32), shape((512, 128), F32)),
        in_specs=[pl.BlockSpec(memory_space=pl.ANY)] * 5,
        out_specs=(VM,) * 3,
        scratch_shapes=[
            buf((4, 1, 4, 128, 128), BF16), buf((32, 108), BF16), buf((64, 864), BF16), buf((64, 1024), BF16),
            buf((128, 384), F32), dma((5,)),
            buf((16, 136, 128), F32), buf((640, 512), F32), buf((4096, 128), F32), buf((640, 1024), BF16),
            buf((512, 640), BF16), buf((128, 1536), BF16), buf((32, 128), BF16), buf((128, 384), BF16),
            buf((256, 1024), F32), buf((128, 1024), BF16), buf((8, 864, 128), F32), buf((1280, 1024), BF16),
            buf((32, 512), F32), buf((1024, 512), BF16), buf((512, 128), F32), buf((64, 1024), BF16),
            buf((864, 128), F32), buf((3, 128, 256), BF16), buf((2, 256, 1024), BF16),
            buf((4, 128, 128), BF16), buf((128, 1024), BF16), buf((64, 1024), BF16),
            buf((1024, 256), BF16), buf((1024, 256), BF16), buf((1008, 256), BF16),
            buf((32, 256), BF16), buf((16, 256), BF16), buf((3, 16, 256), BF16), buf((16, 256), BF16),
            buf((15, 16, 256), BF16), buf((16, 256), BF16),
            dma((2,)), dma((2,)), dma((2,)), dma((8, 2)), dma((2,)), dma((2,)), dma((2,)), dma((2,)), dma((2,)),
            dma, dma((4,)), dma((4, 2)), dma((2,)),
        ],
        compiler_params=pltpu.CompilerParams(
            vmem_limit_bytes=VMEM_CAP, collective_id=0, has_side_effects=True
        ),
    )(volume, kernel_one.T, kernel_two.T, cotangent.reshape(64, 1024), tap_matrix())
    features, in_one, in_two, out_one, out_two, w_one, w_two = pl.pallas_call(
        unpack_kernel,
        name="unpack",
        out_shape=(
            shape((64, 1, 16, 64), BF16), shape((108, 108), F32), shape((864, 864), F32), shape((32, 32), F32),
            shape((64, 64), F32), shape((32, 108), F32), shape((64, 864), F32),
        ),
        in_specs=[VM] * 3,
        out_specs=(VM, VM, pl.BlockSpec(memory_space=pl.ANY), VM, VM, VM, VM),
        scratch_shapes=[buf((864, 864), F32), dma((7,))],
        compiler_params=pltpu.CompilerParams(vmem_limit_bytes=VMEM_CAP),
    )(sums, late, feat)
    return features.transpose(0, 1, 3, 2), in_one, in_two, out_one, out_two, w_one.T, w_two.T


def solution(mesh):
    placed = (P(None, "batch", "space", None, None), P(), P(), P(None, "batch", "space", None))
    return jax.shard_map(
        local,
        mesh=mesh,
        in_specs=placed,
        out_specs=(P(None, "batch", None, "space"), P(), P(), P(), P(), P(), P()),
        check_vma=False,
    )
```

```python
import math

import jax
import jax.numpy as jnp
import numpy as np
from jax import lax
from jax.experimental import pallas as pl
from jax.experimental.pallas import tpu as pltpu
from jax.sharding import PartitionSpec as P

F32 = jnp.float32
BF16 = jnp.bfloat16
VMEM_CAP = 56 * 1024 * 1024
TOTAL_ONE = 2 * 128 * 64 * 64
TOTAL_TWO = 2 * 64 * 32 * 32


def tap_matrix():
    table = np.zeros((128, 3, 128), np.float32)
    for c in range(4):
        for a in range(3):
            for b in range(3):
                for e in range(3):
                    table[c * 27 + a * 9 + b * 3 + e, a, e * 20 + c * 5 + b] = 1
    return jnp.asarray(table.reshape(128, 384), F32)


def gelu_parts(value):
    square = value * value
    tangent = jnp.tanh(0.7978845608028654 * (value + 0.044715 * value * square))
    half = 0.5 * (1.0 + tangent)
    slope = half + 0.5 * value * (1.0 - tangent * tangent) * 0.7978845608028654 * (1.0 + 3.0 * 0.044715 * square)
    return value * half, slope


def dot(a, b):
    return lax.dot_general(a, b, (((1,), (0,)), ((), ())), preferred_element_type=F32)


def dot_nt(a, b):
    return lax.dot_general(a, b, (((1,), (1,)), ((), ())), preferred_element_type=F32)


def halves(value):
    high = value.astype(BF16)
    return high, (value - high.astype(F32)).astype(BF16)


VM = pl.BlockSpec(memory_space=pltpu.VMEM)
MESH = pl.DeviceIdType.MESH


def shifted(me, k):
    return (((me & 48) + (k & 48)) & 48) | (((me & 12) + (k & 12)) & 12) | (((me & 3) + (k & 3)) & 3)


def rows(index, count=16):
    return pl.ds(pl.multiple_of(index * count, count), count)


def await_bytes(ref, sem):
    pltpu.make_async_copy(ref, ref, sem).wait()


def spread_planes(first, count, load, vf, lf, of, uu, ee):
    def split(zz, carry):
        for c in range(4):
            at = zz * 4 + c
            vf[at, 8:136, :] = load(c, zz)
            for res in range(5):
                row = pl.ds(pl.multiple_of(at * 40 + res * 8, 8), 8)
                for m in range(4):
                    lf[row, m * 128 : (m + 1) * 128] = vf[at, pl.ds(7 + 4 * m + res, 8, stride=16), :]
        return carry

    lax.fori_loop(0, count, split, 0)
    parts = dot(lf[0 : count * 160, :].astype(BF16), ee[...])
    for zz in range(count):
        for res in range(5):
            of[zz * 1024 + res * 160 : zz * 1024 + (res + 1) * 160, :] = parts[
                zz * 160 : (zz + 1) * 160, res * 128 : (res + 1) * 128
            ]

    def flatten(zz, carry):
        for group in range(7):
            for j in range(8):
                start = zz * 1024 + group * 128 + j
                part = jnp.concatenate(
                    [of[pl.ds(start, 8, stride=8), :], of[pl.ds(start + 64, 8, stride=8), :]], axis=0
                )
                at = pl.ds(pl.multiple_of((first + zz) * 128 + group * 16, 16), 16)
                uu[at, j * 128 : (j + 1) * 128] = part.astype(BF16)
        uu[pl.ds(pl.multiple_of((first + zz) * 128 + 112, 16), 16), :] = jnp.zeros((16, 1024), BF16)
        return carry

    lax.fori_loop(0, count, flatten, 0)


def place_taps(act, a, p2f):
    lane = lax.broadcasted_iota(jnp.int32, (1, 1024), 1)
    for b in range(3):
        for e in range(3):
            p, q = (b + 1) % 2, (e + 1) % 2
            block = act[(p * 2 + q) * 32 : (p * 2 + q + 1) * 32, :]
            if e == 0:
                block = jnp.where(lane % 32 == 0, 0.0, pltpu.roll(block, 1, 1))
            if b == 0:
                block = jnp.where(lane < 32, 0.0, pltpu.roll(block, 32, 1))
            for j in range(8):
                p2f[j, pl.ds(a * 9 + b * 3 + e, 32, stride=27), :] = block[:, j * 128 : (j + 1) * 128]


def first_factor(uu, taps, tiles):
    gram = dot_nt(uu[0:384, :], uu[0:384, :]) + dot_nt(uu[256:640, :], uu[256:640, :])
    total = jnp.zeros((128, 128), F32)
    for part in halves(gram):
        for pq in range(4):
            tap = taps[:, pq * 384 : (pq + 1) * 384]
            total = total + dot(tap, dot_nt(part, tap).astype(BF16))
    total = total * (1.0 / TOTAL_ONE)
    for k in range(4):
        tiles[:, k * 128 : (k + 1) * 128] = total[k * 32 : (k + 1) * 32, :]


def group_matrix(half_tile, pick):
    lane = lax.broadcasted_iota(jnp.int32, (128, 128), 0) - half_tile * 64
    col = lax.broadcasted_iota(jnp.int32, (128, 128), 1)
    for low in range(8):
        inside = (col >= low * 16) & (col < (low + 1) * 16)
        for x in range(4):
            hit = inside & (lane == x * 16 + col - low * 16)
            pick[low * 128 : (low + 1) * 128, x * 128 : (x + 1) * 128] = jnp.where(hit, 1.0, 0.0).astype(BF16)


def backward_weights(k2_ref, k2f, aa):
    k2f[:, 0:64] = k2_ref[...].astype(F32).T
    aa[...] = jnp.zeros((3, 128, 256), BF16)
    for a in range(3):
        for b in range(3):
            for e in range(3):
                p, q = (b + 1) % 2, (e + 1) % 2
                sy, sx = int(b == 0), int(e == 0)
                block = k2f[pl.ds(a * 9 + b * 3 + e, 32, stride=27), :]
                at = (p * 2 + q) * 32
                aa[a, at : at + 32, (sy * 2 + sx) * 64 : (sy * 2 + sx + 1) * 64] = block[:, 0:64].astype(BF16)


def layer_two_part(aa, a, plane):
    lane = lax.broadcasted_iota(jnp.int32, (1, 1024), 1)
    parts = lax.dot_general(aa[a], plane, (((0,), (0,)), ((), ())), preferred_element_type=F32)
    low = parts[0:64] + jnp.where(lane % 32 == 0, 0.0, pltpu.roll(parts[64:128], 1, 1))
    high = parts[128:192] + jnp.where(lane % 32 == 0, 0.0, pltpu.roll(parts[192:256], 1, 1))
    return low + jnp.where(lane < 32, 0.0, pltpu.roll(high, 32, 1))


def shift_back(value, gs, n):
    lane = lax.broadcasted_iota(jnp.int32, (1, 1024), 1)
    for sy in range(2):
        for sx in range(2):
            moved = value
            if sx:
                moved = jnp.where(lane % 32 == 31, 0.0, pltpu.roll(moved, 1023, 1))
            if sy:
                moved = jnp.where(lane >= 992, 0.0, pltpu.roll(moved, 992, 1))
            gs[n, (sy * 2 + sx) * 64 : (sy * 2 + sx + 1) * 64, :] = moved.astype(BF16)


def step_kernel(
    vol_hbm, k1_hbm, k2_hbm, cot_hbm, tap_hbm, out_ref, late_out_ref, feat_out_ref,
    vol_ref, k1_ref, k2_ref, cot_ref, tap_ref, load_sem, vf, lf, of, uu, ee, taps, k1p, ww, slopes, hid, pre_two, p2f, p2b, tiles, sums, feat, feat_near, feat_mid, feat_far, pick, g2, k2f, aa, gs,
    rim, hid_in, g2_in, pair, half, got, late, late_pair, late_x, late_sum, late_yz, late_total,
    rim_sem, hid_sem, g2_sem, pair_sem, late_pair_sem, rs_sem, feat_sem, far_sem, x_sem, yz_sem,
    gather_send, gather_recv, back_sem, late_back_sem,
):
    me, core = lax.axis_index("space"), lax.axis_index("batch")
    sibling = (me, 1 - core)
    above, below = (lax.rem(me + 1, 64), core), (lax.rem(me + 63, 64), core)
    mine = pl.ds(pl.multiple_of(core * 256, 256), 256)
    other = pl.ds(pl.multiple_of((1 - core) * 256, 256), 256)

    def send(src, dst, sems, to):
        copy = pltpu.make_async_remote_copy(
            src_ref=src, dst_ref=dst, send_sem=sems.at[0], recv_sem=sems.at[1], device_id=to, device_id_type=MESH
        )
        copy.start()
        return copy

    barrier = pltpu.get_barrier_semaphore()
    pl.semaphore_signal(barrier, inc=1, device_id=sibling, device_id_type=MESH)

    for k in range(1, 64):
        pl.semaphore_signal(barrier, inc=1, device_id=(shifted(me, k), core), device_id_type=MESH)
    loads = [
        pltpu.make_async_copy(src, dst, load_sem.at[n])
        for n, (src, dst) in enumerate(
            ((vol_hbm, vol_ref), (tap_hbm, tap_ref), (k1_hbm, k1_ref), (k2_hbm, k2_ref), (cot_hbm, cot_ref))
        )
    ]
    for load in loads:
        load.start()

    at_x = lax.broadcasted_iota(jnp.int32, (128, 128), 0)
    lane = lax.broadcasted_iota(jnp.int32, (128, 128), 1)
    for m in range(4):
        for res in range(5):
            hit = (at_x == 4 * (lane - 32 * m) + (res - 1)) & (lane >= 32 * m) & (lane < 32 * (m + 1))
            ee[m * 128 : (m + 1) * 128, res * 128 : (res + 1) * 128] = jnp.where(hit, 1.0, 0.0).astype(BF16)
    vf[:, 0:8, :] = jnp.zeros((16, 8, 128), F32)
    for zz in range(4):
        of[zz * 1024 + 800 : zz * 1024 + 896, :] = jnp.zeros((96, 128), F32)
    for load in loads:
        load.wait()
    for pq, step in enumerate((0, 40, 2, 42)):
        moved = tap_ref[...] if step == 0 else pltpu.roll(tap_ref[...], step, 1)
        taps[:, pq * 384 : (pq + 1) * 384] = moved.astype(BF16)
    k1p[...] = jnp.zeros((32, 128), BF16)
    k1p[:, 0:108] = k1_ref[...]
    wide = dot(k1p[...], taps[...])
    for pq in range(4):
        ww[pq * 32 : (pq + 1) * 32, :] = wide[:, pq * 384 : (pq + 1) * 384].astype(BF16)

    pl.semaphore_wait(barrier, 64)
    rim_copy = send(vol_ref.at[:, 0, 3], rim, rim_sem, above)

    spread_planes(1, 4, lambda c, zz: vol_ref[c, 0, zz].astype(F32), vf, lf, of, uu, ee)
    act, slope = gelu_parts(dot(ww[...], uu[256:640, :]))
    slopes[128:256, :] = slope
    hid[...] = act.astype(BF16)
    hid_copy = send(hid, hid_in, hid_sem, above)
    place_taps(hid[...].astype(F32), 2, p2f)
    backward_weights(k2_ref, k2f, aa)
    pre_two[...] = layer_two_part(aa, 2, hid[...])

    group_matrix((me // 4) & 1, pick)

    rim_copy.wait()
    spread_planes(
        0, 1, lambda c, zz: jnp.where(me > 0, rim[c].astype(F32), 0.0), vf, lf, of, uu, ee
    )
    act, slope = gelu_parts(dot(ww[...], uu[0:384, :]))
    slopes[0:128, :] = slope
    act = act.astype(BF16)
    place_taps(act.astype(F32), 1, p2f)
    pre_two[...] += layer_two_part(aa, 1, act)
    first_factor(uu, taps, tiles)

    hid_copy.wait()
    lower = jnp.where(me > 0, hid_in[...].astype(F32), 0.0)
    act, slope = gelu_parts(pre_two[...] + layer_two_part(aa, 0, lower.astype(BF16)))
    g2[...] = (cot_ref[...].astype(F32) * (1.0 / math.sqrt(TOTAL_TWO)) * slope).astype(BF16)
    g2_copy = send(g2, g2_in, g2_sem, below)

    feat[...] = act.astype(BF16)
    plane = me // 4
    half_tile = plane & 1

    @pl.loop(1, 16)
    def _(k):
        to = shifted(me, 4 * k)
        tile = pl.ds(pl.multiple_of((to // 8) * 128, 128), 128)
        send(feat.at[:, tile], feat_near.at[plane], feat_sem, (to, core))

    feat_near[plane] = feat[:, pl.ds(pl.multiple_of((me // 8) * 128, 128), 128)]

    place_taps(lower, 0, p2f)
    for j in range(8):
        p2b[0:864, j * 128 : (j + 1) * 128] = p2f[j].astype(BF16)
    p2b[864:896, :] = jnp.zeros((32, 1024), BF16)
    p2b[896:1280, :] = p2b[0:384, :]

    def gram_part(side):
        lanes = pl.ds(pl.multiple_of(side * 256, 256), 256)
        for i in range(7):
            cols = pl.ds(pl.multiple_of(i * 128 + side * 256, 128), 256)
            block = dot_nt(p2b[i * 128 : (i + 1) * 128, :], p2b[cols, :]) * (1.0 / TOTAL_TWO)
            sums[i * 128 : (i + 1) * 128, lanes] = block.astype(BF16)
        sums[864:896, lanes] = tiles[:, lanes].astype(BF16)

    grads = dot_nt(g2[...], p2b[0:896, :])
    own = dot_nt(g2[...], g2[...])
    sums[896:960, :] = grads[:, 0:512].astype(BF16)
    sums[960:1024, 0:384] = grads[:, 512:896].astype(BF16)
    sums[960:1024, 384:512] = jnp.concatenate([own, jnp.zeros((64, 64), F32)], axis=1).astype(BF16)
    gram_part(1 - core)
    pair_copy = send(sums.at[:, other], pair, pair_sem, sibling)
    gram_part(core)
    pair_copy.wait()
    half[...] = (sums[:, mine].astype(F32) + pair[...].astype(F32)).astype(BF16)

    def scatter(k, carry):
        to = shifted(me, k)
        send(half.at[rows(to), :], got.at[rows(k - 1), :], rs_sem, (to, core))
        return carry

    lax.fori_loop(1, 64, scatter, 0)

    for sem in (feat_sem.at[0], feat_sem.at[1]):
        await_bytes(feat_near.at[0:15], sem)
    for k in range(16):
        feat_mid[k * 64 : (k + 1) * 64, :] = feat_near[k].astype(F32)
    wide = jnp.concatenate([feat_mid[pl.ds(low, 128, stride=8), :] for low in range(8)], axis=1).astype(BF16)
    wide = dot(wide, pick[...]).astype(BF16)
    for x in range(4):
        feat_far[x] = wide[:, x * 128 : (x + 1) * 128]
    for k in range(1, 4):
        to = shifted(me, k)
        send(feat_far.at[to & 3], feat_out_ref.at[me & 3], far_sem, (to, core))
    feat_out_ref[me & 3] = feat_far[me & 3]

    shift_back(g2[...].astype(F32), gs, 0)
    g2_copy.wait()
    shift_back(jnp.where(me < 63, g2_in[...].astype(F32), 0.0), gs, 1)
    cross = jnp.zeros((128, 384), F32)
    gram = jnp.zeros((128, 128), F32)
    for h in range(2):
        spread = dot(aa[h + 1], gs[0])
        if h == 1:
            spread = spread + dot(aa[0], gs[1])
        g1 = (spread * slopes[h * 128 : (h + 1) * 128, :]).astype(BF16)
        cross = cross + dot_nt(g1, uu[h * 256 : h * 256 + 384, :])
        gram = gram + dot_nt(g1, g1)
    weight = jnp.zeros((32, 128), F32)
    own = jnp.zeros((32, 32), F32)
    for pq in range(4):
        for part in halves(cross[pq * 32 : (pq + 1) * 32, :]):
            weight = weight + dot_nt(part, taps[:, pq * 384 : (pq + 1) * 384])
        own = own + gram[pq * 32 : (pq + 1) * 32, pq * 32 : (pq + 1) * 32]
    late[:, 0:128] = weight.astype(BF16)
    late[:, 128:256] = jnp.concatenate([own, jnp.zeros((32, 96), F32)], axis=1).astype(BF16)
    send(late.at[rows(1 - core), :], late_pair, late_pair_sem, sibling).wait()
    late_sum[...] = (late[rows(core), :].astype(F32) + late_pair[...].astype(F32)).astype(BF16)
    for k in range(1, 4):
        send(late_sum, late_x.at[k - 1], x_sem, (shifted(me, k), core))
    await_bytes(late_x, x_sem.at[0])
    await_bytes(late_x, x_sem.at[1])
    near = late_sum[...].astype(F32) + late_x[0].astype(F32) + (late_x[1].astype(F32) + late_x[2].astype(F32))
    late_total[...] = near.astype(BF16)
    for k in range(1, 16):
        send(late_total, late_yz.at[k - 1], yz_sem, (shifted(me, 4 * k), core))

    await_bytes(got, rs_sem.at[1])
    parts = [half[rows(me), :].astype(F32), jnp.zeros((16, 256), F32)]
    for k in range(63):
        parts[k % 2] = parts[k % 2] + got[k * 16 : (k + 1) * 16, :].astype(F32)
    out_ref[rows(me), mine] = (parts[0] + parts[1]).astype(BF16)

    def gather(k, carry):
        piece = out_ref.at[rows(me), mine]
        copy = pltpu.make_async_remote_copy(
            src_ref=piece, dst_ref=piece, send_sem=gather_send, recv_sem=gather_recv.at[k // 16],
            device_id=(shifted(me, k), core), device_id_type=MESH,
        )
        copy.start()
        return carry

    lax.fori_loop(1, 64, gather, 0)

    backs = []
    for k in range(4):
        count = 240 if k == 0 else 256
        await_bytes(half.at[0:count, :], gather_recv.at[k])
        block = pl.ds(pl.multiple_of(lax.rem(me // 16 + 4 - k, 4) * 256, 256), 256)
        backs.append(send(out_ref.at[block, mine], out_ref.at[block, mine], back_sem.at[k], sibling))
    await_bytes(late_yz, yz_sem.at[0])
    await_bytes(late_yz, yz_sem.at[1])
    far = late_total[...].astype(F32)
    for k in range(15):
        far = far + late_yz[k].astype(F32)
    late_out_ref[rows(core), :] = far
    backs.append(send(late_out_ref.at[rows(core), :], late_out_ref.at[rows(core), :], late_back_sem, sibling))
    await_bytes(got, rs_sem.at[0])
    await_bytes(got, gather_send)
    for sem in (far_sem.at[0], far_sem.at[1]):
        await_bytes(feat_far.at[0:3], sem)
    for copy in backs:
        copy.wait()


def unpack_kernel(
    sums_ref, late_ref, feat_ref,
    features_ref, in_one_ref, in_two_hbm, out_one_ref, out_two_ref, w_one_ref, w_two_ref, in_two, feat, store_sem,
):
    stores = []
    row = lax.broadcasted_iota(jnp.int32, (128, 128), 0)
    eye = jnp.where(row == lax.broadcasted_iota(jnp.int32, (128, 128), 1), 1.0, 0.0).astype(BF16)
    for i in range(7):
        height = min(128, 864 - i * 128)
        band = slice(i * 128, i * 128 + height)
        for k in range(-3, 4):
            j = (i + k) % 7
            width = min(128, 864 - j * 128)
            if k >= 0:
                block = sums_ref[i * 128 : (i + 1) * 128, k * 128 : (k + 1) * 128].astype(F32)
            else:
                block = dot_nt(eye, sums_ref[j * 128 : (j + 1) * 128, -k * 128 : (1 - k) * 128])
            in_two[band, j * 128 : j * 128 + width] = block[0:height, 0:width]
        stores.append(pltpu.make_async_copy(in_two.at[band, :], in_two_hbm.at[band, :], store_sem.at[i]))
        stores[-1].start()
    w_two_ref[:, 0:512] = sums_ref[896:960, :].astype(F32)
    rest = sums_ref[960:1024, :].astype(F32)
    w_two_ref[:, 512:864] = rest[:, 0:352]
    out_two_ref[...] = rest[:, 384:448]
    first = sums_ref[864:896, :].astype(F32)
    for k in range(4):
        height = min(32, 108 - k * 32)
        in_one_ref[k * 32 : k * 32 + height, :] = first[0:height, k * 128 : k * 128 + 108]
    late = late_ref[...]
    w_one_ref[...] = late[:, 0:108]
    out_one_ref[...] = late[:, 128:160]
    for x in range(4):
        plane = feat_ref[x].astype(F32)
        for yz in range(16):
            at = (yz * 4 + x) * 8
            feat[at : at + 8, :] = plane[yz * 8 : (yz + 1) * 8, :]
    for r in range(8):
        block = feat[pl.ds(r, 64, stride=8), :]
        features_ref[r * 8 : (r + 1) * 8, 0, :, :] = dot_nt(eye, block.astype(BF16)).reshape(8, 16, 64).astype(BF16)
    for store in stores:
        store.wait()


def local(volume, kernel_one, kernel_two, cotangent):
    shape = jax.ShapeDtypeStruct
    dma = pltpu.SemaphoreType.DMA
    buf = pltpu.VMEM
    sums, late, feat = pl.pallas_call(
        step_kernel,
        name="step",
        out_shape=(shape((1024, 512), BF16), shape((32, 256), F32), shape((4, 128, 128), BF16)),
        in_specs=[pl.BlockSpec(memory_space=pl.ANY)] * 5,
        out_specs=(VM,) * 3,
        scratch_shapes=[
            buf((4, 1, 4, 128, 128), BF16), buf((32, 108), BF16), buf((64, 864), BF16), buf((64, 1024), BF16),
            buf((128, 384), F32), dma((5,)),
            buf((16, 136, 128), F32), buf((640, 512), F32), buf((4096, 128), F32), buf((640, 1024), BF16),
            buf((512, 640), BF16), buf((128, 1536), BF16), buf((32, 128), BF16), buf((128, 384), BF16),
            buf((256, 1024), F32), buf((128, 1024), BF16), buf((64, 1024), F32), buf((8, 864, 128), F32), buf((1280, 1024), BF16),
            buf((32, 512), F32), buf((1024, 512), BF16), buf((64, 1024), BF16), buf((16, 64, 128), BF16), buf((1024, 128), F32),
            buf((4, 128, 128), BF16), buf((1024, 512), BF16), buf((64, 1024), BF16),
            buf((864, 128), F32), buf((3, 128, 256), BF16), buf((2, 256, 1024), BF16),
            buf((4, 128, 128), BF16), buf((128, 1024), BF16), buf((64, 1024), BF16),
            buf((1024, 256), BF16), buf((1024, 256), BF16), buf((1008, 256), BF16),
            buf((32, 256), BF16), buf((16, 256), BF16), buf((3, 16, 256), BF16), buf((16, 256), BF16),
            buf((15, 16, 256), BF16), buf((16, 256), BF16),
            dma((2,)), dma((2,)), dma((2,)), dma((2,)), dma((2,)), dma((2,)), dma((2,)), dma((2,)), dma((2,)), dma((2,)),
            dma, dma((4,)), dma((4, 2)), dma((2,)),
        ],
        compiler_params=pltpu.CompilerParams(
            vmem_limit_bytes=VMEM_CAP, collective_id=0, has_side_effects=True
        ),
    )(volume, kernel_one.T, kernel_two.T, cotangent.reshape(64, 1024), tap_matrix())
    features, in_one, in_two, out_one, out_two, w_one, w_two = pl.pallas_call(
        unpack_kernel,
        name="unpack",
        out_shape=(
            shape((64, 1, 16, 64), BF16), shape((108, 108), F32), shape((864, 864), F32), shape((32, 32), F32),
            shape((64, 64), F32), shape((32, 108), F32), shape((64, 864), F32),
        ),
        in_specs=[VM] * 3,
        out_specs=(VM, VM, pl.BlockSpec(memory_space=pl.ANY), VM, VM, VM, VM),
        scratch_shapes=[buf((864, 864), F32), buf((512, 128), F32), dma((7,))],
        compiler_params=pltpu.CompilerParams(vmem_limit_bytes=VMEM_CAP),
    )(sums, late, feat)
    return features.transpose(0, 1, 3, 2), in_one, in_two, out_one, out_two, w_one.T, w_two.T


def solution(mesh):
    placed = (P(None, "batch", "space", None, None), P(), P(), P(None, "batch", "space", None))
    return jax.shard_map(
        local,
        mesh=mesh,
        in_specs=placed,
        out_specs=(P(None, "batch", None, "space"), P(), P(), P(), P(), P(), P()),
        check_vma=False,
    )
```

```python
import math

import jax
import jax.numpy as jnp
import numpy as np
from jax import lax
from jax.experimental import pallas as pl
from jax.experimental.pallas import tpu as pltpu
from jax.sharding import PartitionSpec as P

F32 = jnp.float32
BF16 = jnp.bfloat16
VMEM_CAP = 56 * 1024 * 1024
TOTAL_ONE = 2 * 128 * 64 * 64
TOTAL_TWO = 2 * 64 * 32 * 32


def tap_matrix():
    table = np.zeros((128, 3, 128), np.float32)
    for c in range(4):
        for a in range(3):
            for b in range(3):
                for e in range(3):
                    table[c * 27 + a * 9 + b * 3 + e, a, e * 20 + c * 5 + b] = 1
    return jnp.asarray(table.reshape(128, 384), F32)


def gelu_parts(value):
    square = value * value
    tangent = jnp.tanh(0.7978845608028654 * (value + 0.044715 * value * square))
    half = 0.5 * (1.0 + tangent)
    slope = half + 0.5 * value * (1.0 - tangent * tangent) * 0.7978845608028654 * (1.0 + 3.0 * 0.044715 * square)
    return value * half, slope


def dot(a, b):
    return lax.dot_general(a, b, (((1,), (0,)), ((), ())), preferred_element_type=F32)


def dot_nt(a, b):
    return lax.dot_general(a, b, (((1,), (1,)), ((), ())), preferred_element_type=F32)


def halves(value):
    high = value.astype(BF16)
    return high, (value - high.astype(F32)).astype(BF16)


VM = pl.BlockSpec(memory_space=pltpu.VMEM)
MESH = pl.DeviceIdType.MESH


def shifted(me, k):
    return (((me & 48) + (k & 48)) & 48) | (((me & 12) + (k & 12)) & 12) | (((me & 3) + (k & 3)) & 3)


def rows(index, count=16):
    return pl.ds(pl.multiple_of(index * count, count), count)


def await_bytes(ref, sem):
    pltpu.make_async_copy(ref, ref, sem).wait()


def spread_planes(first, count, load, vf, lf, of, uu, ee):
    def split(zz, carry):
        for c in range(4):
            at = zz * 4 + c
            vf[at, 8:136, :] = load(c, zz)
            for res in range(5):
                row = pl.ds(pl.multiple_of(at * 40 + res * 8, 8), 8)
                for m in range(4):
                    lf[row, m * 128 : (m + 1) * 128] = vf[at, pl.ds(7 + 4 * m + res, 8, stride=16), :]
        return carry

    lax.fori_loop(0, count, split, 0)
    parts = dot(lf[0 : count * 160, :].astype(BF16), ee[...])
    for zz in range(count):
        for res in range(5):
            of[zz * 1024 + res * 160 : zz * 1024 + (res + 1) * 160, :] = parts[
                zz * 160 : (zz + 1) * 160, res * 128 : (res + 1) * 128
            ]

    def flatten(zz, carry):
        for group in range(7):
            for j in range(8):
                start = zz * 1024 + group * 128 + j
                part = jnp.concatenate(
                    [of[pl.ds(start, 8, stride=8), :], of[pl.ds(start + 64, 8, stride=8), :]], axis=0
                )
                at = pl.ds(pl.multiple_of((first + zz) * 128 + group * 16, 16), 16)
                uu[at, j * 128 : (j + 1) * 128] = part.astype(BF16)
        uu[pl.ds(pl.multiple_of((first + zz) * 128 + 112, 16), 16), :] = jnp.zeros((16, 1024), BF16)
        return carry

    lax.fori_loop(0, count, flatten, 0)


def place_taps(act, a, p2f):
    lane = lax.broadcasted_iota(jnp.int32, (1, 1024), 1)
    for b in range(3):
        for e in range(3):
            p, q = (b + 1) % 2, (e + 1) % 2
            block = act[(p * 2 + q) * 32 : (p * 2 + q + 1) * 32, :]
            if e == 0:
                block = jnp.where(lane % 32 == 0, 0.0, pltpu.roll(block, 1, 1))
            if b == 0:
                block = jnp.where(lane < 32, 0.0, pltpu.roll(block, 32, 1))
            for j in range(8):
                p2f[j, pl.ds(a * 9 + b * 3 + e, 32, stride=27), :] = block[:, j * 128 : (j + 1) * 128]


def first_factor(uu, taps, tiles):
    gram = dot_nt(uu[0:384, :], uu[0:384, :]) + dot_nt(uu[256:640, :], uu[256:640, :])
    total = jnp.zeros((128, 128), F32)
    for part in halves(gram):
        for pq in range(4):
            tap = taps[:, pq * 384 : (pq + 1) * 384]
            total = total + dot(tap, dot_nt(part, tap).astype(BF16))
    total = total * (1.0 / TOTAL_ONE)
    for k in range(4):
        tiles[:, k * 128 : (k + 1) * 128] = total[k * 32 : (k + 1) * 32, :]


def group_matrix(half_tile, pick):
    lane = lax.broadcasted_iota(jnp.int32, (128, 128), 0) - half_tile * 64
    col = lax.broadcasted_iota(jnp.int32, (128, 128), 1)
    for low in range(8):
        inside = (col >= low * 16) & (col < (low + 1) * 16)
        for x in range(4):
            hit = inside & (lane == x * 16 + col - low * 16)
            pick[low * 128 : (low + 1) * 128, x * 128 : (x + 1) * 128] = jnp.where(hit, 1.0, 0.0).astype(BF16)


def backward_weights(k2_ref, k2f, aa):
    k2f[:, 0:64] = k2_ref[...].astype(F32).T
    aa[...] = jnp.zeros((3, 128, 256), BF16)
    for a in range(3):
        for b in range(3):
            for e in range(3):
                p, q = (b + 1) % 2, (e + 1) % 2
                sy, sx = int(b == 0), int(e == 0)
                block = k2f[pl.ds(a * 9 + b * 3 + e, 32, stride=27), :]
                at = (p * 2 + q) * 32
                aa[a, at : at + 32, (sy * 2 + sx) * 64 : (sy * 2 + sx + 1) * 64] = block[:, 0:64].astype(BF16)


def layer_two_part(aa, a, plane):
    lane = lax.broadcasted_iota(jnp.int32, (1, 1024), 1)
    parts = lax.dot_general(aa[a], plane, (((0,), (0,)), ((), ())), preferred_element_type=F32)
    low = parts[0:64] + jnp.where(lane % 32 == 0, 0.0, pltpu.roll(parts[64:128], 1, 1))
    high = parts[128:192] + jnp.where(lane % 32 == 0, 0.0, pltpu.roll(parts[192:256], 1, 1))
    return low + jnp.where(lane < 32, 0.0, pltpu.roll(high, 32, 1))


def shift_back(value, gs, n):
    lane = lax.broadcasted_iota(jnp.int32, (1, 1024), 1)
    for sy in range(2):
        for sx in range(2):
            moved = value
            if sx:
                moved = jnp.where(lane % 32 == 31, 0.0, pltpu.roll(moved, 1023, 1))
            if sy:
                moved = jnp.where(lane >= 992, 0.0, pltpu.roll(moved, 992, 1))
            gs[n, (sy * 2 + sx) * 64 : (sy * 2 + sx + 1) * 64, :] = moved.astype(BF16)


def step_kernel(
    vol_hbm, k1_hbm, k2_hbm, cot_hbm, tap_hbm, out_hbm, late_hbm, feat_hbm,
    vol_ref, k1_ref, k2_ref, cot_ref, tap_ref, load_sem, vf, lf, of, uu, ee, taps, k1p, ww, slopes, hid, pre_two, p2f, p2b, tiles, sums, feat, feat_near, feat_mid, feat_far, pick, g2, k2f, aa, gs,
    rim, hid_in, g2_in, pair, half, got, piece, late, late_pair, late_x, late_sum, late_yz, late_total, late_far,
    rim_sem, hid_sem, g2_sem, pair_sem, late_pair_sem, rs_send, rs_recv, feat_sem, far_sem, x_sem, yz_sem,
    gather_send, gather_recv, back_sem, late_back_sem, keep_sem,
):
    me, core = lax.axis_index("space"), lax.axis_index("batch")
    sibling = (me, 1 - core)
    above, below = (lax.rem(me + 1, 64), core), (lax.rem(me + 63, 64), core)
    mine = pl.ds(pl.multiple_of(core * 256, 256), 256)
    other = pl.ds(pl.multiple_of((1 - core) * 256, 256), 256)

    def send(src, dst, sems, to):
        copy = pltpu.make_async_remote_copy(
            src_ref=src, dst_ref=dst, send_sem=sems.at[0], recv_sem=sems.at[1], device_id=to, device_id_type=MESH
        )
        copy.start()
        return copy

    barrier = pltpu.get_barrier_semaphore()
    pl.semaphore_signal(barrier, inc=1, device_id=sibling, device_id_type=MESH)

    for k in range(1, 64):
        pl.semaphore_signal(barrier, inc=1, device_id=(shifted(me, k), core), device_id_type=MESH)
    loads = [
        pltpu.make_async_copy(src, dst, load_sem.at[n])
        for n, (src, dst) in enumerate(
            ((vol_hbm, vol_ref), (tap_hbm, tap_ref), (k1_hbm, k1_ref), (k2_hbm, k2_ref), (cot_hbm, cot_ref))
        )
    ]
    for load in loads:
        load.start()

    at_x = lax.broadcasted_iota(jnp.int32, (128, 128), 0)
    lane = lax.broadcasted_iota(jnp.int32, (128, 128), 1)
    for m in range(4):
        for res in range(5):
            hit = (at_x == 4 * (lane - 32 * m) + (res - 1)) & (lane >= 32 * m) & (lane < 32 * (m + 1))
            ee[m * 128 : (m + 1) * 128, res * 128 : (res + 1) * 128] = jnp.where(hit, 1.0, 0.0).astype(BF16)
    vf[:, 0:8, :] = jnp.zeros((16, 8, 128), F32)
    for zz in range(4):
        of[zz * 1024 + 800 : zz * 1024 + 896, :] = jnp.zeros((96, 128), F32)
    for load in loads:
        load.wait()
    for pq, step in enumerate((0, 40, 2, 42)):
        moved = tap_ref[...] if step == 0 else pltpu.roll(tap_ref[...], step, 1)
        taps[:, pq * 384 : (pq + 1) * 384] = moved.astype(BF16)
    k1p[...] = jnp.zeros((32, 128), BF16)
    k1p[:, 0:108] = k1_ref[...]
    wide = dot(k1p[...], taps[...])
    for pq in range(4):
        ww[pq * 32 : (pq + 1) * 32, :] = wide[:, pq * 384 : (pq + 1) * 384].astype(BF16)

    pl.semaphore_wait(barrier, 64)
    rim_copy = send(vol_ref.at[:, 0, 3], rim, rim_sem, above)

    spread_planes(1, 4, lambda c, zz: vol_ref[c, 0, zz].astype(F32), vf, lf, of, uu, ee)
    act, slope = gelu_parts(dot(ww[...], uu[256:640, :]))
    slopes[128:256, :] = slope
    hid[...] = act.astype(BF16)
    hid_copy = send(hid, hid_in, hid_sem, above)
    place_taps(hid[...].astype(F32), 2, p2f)
    backward_weights(k2_ref, k2f, aa)
    pre_two[...] = layer_two_part(aa, 2, hid[...])

    group_matrix((me // 4) & 1, pick)

    rim_copy.wait()
    spread_planes(
        0, 1, lambda c, zz: jnp.where(me > 0, rim[c].astype(F32), 0.0), vf, lf, of, uu, ee
    )
    act, slope = gelu_parts(dot(ww[...], uu[0:384, :]))
    slopes[0:128, :] = slope
    act = act.astype(BF16)
    place_taps(act.astype(F32), 1, p2f)
    pre_two[...] += layer_two_part(aa, 1, act)
    first_factor(uu, taps, tiles)

    hid_copy.wait()
    lower = jnp.where(me > 0, hid_in[...].astype(F32), 0.0)
    act, slope = gelu_parts(pre_two[...] + layer_two_part(aa, 0, lower.astype(BF16)))
    g2[...] = (cot_ref[...].astype(F32) * (1.0 / math.sqrt(TOTAL_TWO)) * slope).astype(BF16)
    g2_copy = send(g2, g2_in, g2_sem, below)

    feat[...] = act.astype(BF16)
    plane = me // 4
    half_tile = plane & 1

    @pl.loop(1, 16)
    def _(k):
        to = shifted(me, 4 * k)
        tile = pl.ds(pl.multiple_of((to // 8) * 128, 128), 128)
        send(feat.at[:, tile], feat_near.at[plane], feat_sem, (to, core))

    feat_near[plane] = feat[:, pl.ds(pl.multiple_of((me // 8) * 128, 128), 128)]

    place_taps(lower, 0, p2f)
    for j in range(8):
        p2b[0:864, j * 128 : (j + 1) * 128] = p2f[j].astype(BF16)
    p2b[864:896, :] = jnp.zeros((32, 1024), BF16)
    p2b[896:1280, :] = p2b[0:384, :]

    def gram_part(side):
        lanes = pl.ds(pl.multiple_of(side * 256, 256), 256)
        for i in range(7):
            cols = pl.ds(pl.multiple_of(i * 128 + side * 256, 128), 256)
            block = dot_nt(p2b[i * 128 : (i + 1) * 128, :], p2b[cols, :]) * (1.0 / TOTAL_TWO)
            sums[i * 128 : (i + 1) * 128, lanes] = block.astype(BF16)
        sums[864:896, lanes] = tiles[:, lanes].astype(BF16)

    def swap_rows(n, block):
        return send(sums.at[block, other], pair.at[block, :], pair_sem.at[n], sibling)

    def add_rows(block):
        half[block, :] = (sums[block, mine].astype(F32) + pair[block, :].astype(F32)).astype(BF16)

    def scatter(k, to):
        copy = pltpu.make_async_remote_copy(
            src_ref=half.at[rows(to), :], dst_ref=got.at[rows(k - 1), :], send_sem=rs_send,
            recv_sem=rs_recv.at[k // 16], device_id=(to, core), device_id_type=MESH,
        )
        copy.start()

    early, late_rows = slice(0, 896), slice(896, 1024)
    gram_part(1 - core)
    pair_copy = swap_rows(0, early)
    gram_part(core)
    pair_copy.wait()
    add_rows(early)

    @pl.loop(1, 64)
    def _(k):
        to = shifted(me, k)

        @pl.when(to < 56)
        def _():
            scatter(k, to)

    grads = dot_nt(g2[...], p2b[0:896, :])
    own = dot_nt(g2[...], g2[...])
    sums[896:960, :] = grads[:, 0:512].astype(BF16)
    sums[960:1024, 0:384] = grads[:, 512:896].astype(BF16)
    sums[960:1024, 384:512] = jnp.concatenate([own, jnp.zeros((64, 64), F32)], axis=1).astype(BF16)
    pair_copy = swap_rows(1, late_rows)
    shift_back(g2[...].astype(F32), gs, 0)
    pair_copy.wait()
    add_rows(late_rows)

    @pl.loop(1, 64)
    def _(k):
        to = shifted(me, k)

        @pl.when(to >= 56)
        def _():
            scatter(k, to)

    for sem in (feat_sem.at[0], feat_sem.at[1]):
        await_bytes(feat_near.at[0:15], sem)
    for k in range(16):
        feat_mid[k * 64 : (k + 1) * 64, :] = feat_near[k].astype(F32)
    wide = jnp.concatenate([feat_mid[pl.ds(low, 128, stride=8), :] for low in range(8)], axis=1).astype(BF16)
    wide = dot(wide, pick[...]).astype(BF16)
    for x in range(4):
        feat_far[x] = wide[:, x * 128 : (x + 1) * 128]
    for k in range(1, 4):
        to = shifted(me, k)
        send(feat_far.at[to & 3], feat_hbm.at[me & 3], far_sem, (to, core))
    feat_keep = pltpu.make_async_copy(feat_far.at[me & 3], feat_hbm.at[me & 3], keep_sem.at[2])
    feat_keep.start()

    g2_copy.wait()
    shift_back(jnp.where(me < 63, g2_in[...].astype(F32), 0.0), gs, 1)
    cross = jnp.zeros((128, 384), F32)
    gram = jnp.zeros((128, 128), F32)
    for h in range(2):
        spread = dot(aa[h + 1], gs[0])
        if h == 1:
            spread = spread + dot(aa[0], gs[1])
        g1 = (spread * slopes[h * 128 : (h + 1) * 128, :]).astype(BF16)
        cross = cross + dot_nt(g1, uu[h * 256 : h * 256 + 384, :])
        gram = gram + dot_nt(g1, g1)
    weight = jnp.zeros((32, 128), F32)
    own = jnp.zeros((32, 32), F32)
    for pq in range(4):
        for part in halves(cross[pq * 32 : (pq + 1) * 32, :]):
            weight = weight + dot_nt(part, taps[:, pq * 384 : (pq + 1) * 384])
        own = own + gram[pq * 32 : (pq + 1) * 32, pq * 32 : (pq + 1) * 32]
    late[:, 0:128] = weight.astype(BF16)
    late[:, 128:256] = jnp.concatenate([own, jnp.zeros((32, 96), F32)], axis=1).astype(BF16)
    send(late.at[rows(1 - core), :], late_pair, late_pair_sem, sibling).wait()
    late_sum[...] = (late[rows(core), :].astype(F32) + late_pair[...].astype(F32)).astype(BF16)
    for k in range(1, 4):
        send(late_sum, late_x.at[k - 1], x_sem, (shifted(me, k), core))
    await_bytes(late_x, x_sem.at[0])
    await_bytes(late_x, x_sem.at[1])
    near = late_sum[...].astype(F32) + late_x[0].astype(F32) + (late_x[1].astype(F32) + late_x[2].astype(F32))
    late_total[...] = near.astype(BF16)
    for k in range(1, 16):
        send(late_total, late_yz.at[k - 1], yz_sem, (shifted(me, 4 * k), core))

    parts = [half[rows(me), :].astype(F32), jnp.zeros((16, 256), F32)]
    for group in range(4):
        slots = range(max(group * 16 - 1, 0), group * 16 + 15)
        await_bytes(got.at[slots[0] * 16 : slots[-1] * 16 + 16, :], rs_recv.at[group])
        for k in slots:
            parts[k % 2] = parts[k % 2] + got[k * 16 : (k + 1) * 16, :].astype(F32)
    piece[...] = (parts[0] + parts[1]).astype(BF16)
    place = out_hbm.at[rows(me), mine]
    keep = pltpu.make_async_copy(piece, place, keep_sem.at[0])
    keep.start()

    @pl.loop(1, 64)
    def _(k):
        copy = pltpu.make_async_remote_copy(
            src_ref=piece, dst_ref=place, send_sem=gather_send, recv_sem=gather_recv.at[k // 16],
            device_id=(shifted(me, k), core), device_id_type=MESH,
        )
        copy.start()

    backs = [feat_keep]
    keep.wait()
    for k in range(4):
        count = 240 if k == 0 else 256
        await_bytes(half.at[0:count, :], gather_recv.at[k])
        block = out_hbm.at[pl.ds(pl.multiple_of(lax.rem(me // 16 + 4 - k, 4) * 256, 256), 256), mine]
        backs.append(send(block, block, back_sem.at[k], sibling))
        if k == 0:
            await_bytes(late_yz, yz_sem.at[0])
            await_bytes(late_yz, yz_sem.at[1])
            far = late_total[...].astype(F32)
            for n in range(15):
                far = far + late_yz[n].astype(F32)
            late_far[...] = far
            place = late_hbm.at[rows(core), :]
            backs.append(pltpu.make_async_copy(late_far, place, keep_sem.at[1]))
            backs[-1].start()
            backs.append(send(late_far, place, late_back_sem, sibling))
    await_bytes(got, rs_send)
    await_bytes(got, gather_send)
    for sem in (far_sem.at[0], far_sem.at[1]):
        await_bytes(feat_far.at[0:3], sem)
    for copy in backs:
        copy.wait()


def unpack_kernel(
    sums_ref, late_ref, feat_ref,
    features_hbm, in_one_hbm, in_two_hbm, out_one_hbm, out_two_hbm, w_one_hbm, w_two_hbm,
    features_ref, in_one_ref, in_two, out_one_ref, out_two_ref, w_one_ref, w_two_ref, feat, store_sem,
):
    def store(src, dst):
        stores.append(pltpu.make_async_copy(src, dst, store_sem.at[len(stores)]))
        stores[-1].start()

    stores = []
    row = lax.broadcasted_iota(jnp.int32, (128, 128), 0)
    eye = jnp.where(row == lax.broadcasted_iota(jnp.int32, (128, 128), 1), 1.0, 0.0).astype(BF16)
    for i in range(7):
        height = min(128, 864 - i * 128)
        band = slice(i * 128, i * 128 + height)
        for k in range(-3, 4):
            j = (i + k) % 7
            width = min(128, 864 - j * 128)
            if k >= 0:
                block = sums_ref[i * 128 : (i + 1) * 128, k * 128 : (k + 1) * 128].astype(F32)
            else:
                block = dot_nt(eye, sums_ref[j * 128 : (j + 1) * 128, -k * 128 : (1 - k) * 128])
            in_two[band, j * 128 : j * 128 + width] = block[0:height, 0:width]
        store(in_two.at[band, :], in_two_hbm.at[band, :])
    w_two_ref[:, 0:512] = sums_ref[896:960, :].astype(F32)
    rest = sums_ref[960:1024, :].astype(F32)
    w_two_ref[:, 512:864] = rest[:, 0:352]
    out_two_ref[...] = rest[:, 384:448]
    first = sums_ref[864:896, :].astype(F32)
    for k in range(4):
        height = min(32, 108 - k * 32)
        in_one_ref[k * 32 : k * 32 + height, :] = first[0:height, k * 128 : k * 128 + 108]
    late = late_ref[...]
    w_one_ref[...] = late[:, 0:108]
    out_one_ref[...] = late[:, 128:160]
    for x in range(4):
        plane = feat_ref[x].astype(F32)
        for yz in range(16):
            at = (yz * 4 + x) * 8
            feat[at : at + 8, :] = plane[yz * 8 : (yz + 1) * 8, :]
    for r in range(8):
        block = feat[pl.ds(r, 64, stride=8), :]
        features_ref[r * 8 : (r + 1) * 8, 0, :, :] = dot_nt(eye, block.astype(BF16)).reshape(8, 16, 64).astype(BF16)
    store(w_two_ref, w_two_hbm)
    store(out_two_ref, out_two_hbm)
    store(in_one_ref, in_one_hbm)
    store(w_one_ref, w_one_hbm)
    store(out_one_ref, out_one_hbm)
    store(features_ref, features_hbm)
    for copy in stores:
        copy.wait()


def local(volume, kernel_one, kernel_two, cotangent):
    shape = jax.ShapeDtypeStruct
    dma = pltpu.SemaphoreType.DMA
    buf = pltpu.VMEM
    sums, late, feat = pl.pallas_call(
        step_kernel,
        name="step",
        out_shape=(shape((1024, 512), BF16), shape((32, 256), F32), shape((4, 128, 128), BF16)),
        in_specs=[pl.BlockSpec(memory_space=pl.ANY)] * 5,
        out_specs=(pl.BlockSpec(memory_space=pl.ANY),) * 3,
        scratch_shapes=[
            buf((4, 1, 4, 128, 128), BF16), buf((32, 108), BF16), buf((64, 864), BF16), buf((64, 1024), BF16),
            buf((128, 384), F32), dma((5,)),
            buf((16, 136, 128), F32), buf((640, 512), F32), buf((4096, 128), F32), buf((640, 1024), BF16),
            buf((512, 640), BF16), buf((128, 1536), BF16), buf((32, 128), BF16), buf((128, 384), BF16),
            buf((256, 1024), F32), buf((128, 1024), BF16), buf((64, 1024), F32), buf((8, 864, 128), F32), buf((1280, 1024), BF16),
            buf((32, 512), F32), buf((1024, 512), BF16), buf((64, 1024), BF16), buf((16, 64, 128), BF16), buf((1024, 128), F32),
            buf((4, 128, 128), BF16), buf((1024, 512), BF16), buf((64, 1024), BF16),
            buf((864, 128), F32), buf((3, 128, 256), BF16), buf((2, 256, 1024), BF16),
            buf((4, 128, 128), BF16), buf((128, 1024), BF16), buf((64, 1024), BF16),
            buf((1024, 256), BF16), buf((1024, 256), BF16), buf((1008, 256), BF16), buf((16, 256), BF16),
            buf((32, 256), BF16), buf((16, 256), BF16), buf((3, 16, 256), BF16), buf((16, 256), BF16),
            buf((15, 16, 256), BF16), buf((16, 256), BF16), buf((16, 256), F32),
            dma((2,)), dma((2,)), dma((2,)), dma((2, 2)), dma((2,)), dma, dma((4,)), dma((2,)), dma((2,)), dma((2,)),
            dma((2,)), dma, dma((4,)), dma((4, 2)), dma((2,)), dma((3,)),
        ],
        compiler_params=pltpu.CompilerParams(
            vmem_limit_bytes=VMEM_CAP, collective_id=0, has_side_effects=True
        ),
    )(volume, kernel_one.T, kernel_two.T, cotangent.reshape(64, 1024), tap_matrix())
    features, in_one, in_two, out_one, out_two, w_one, w_two = pl.pallas_call(
        unpack_kernel,
        name="unpack",
        out_shape=(
            shape((64, 1, 16, 64), BF16), shape((108, 108), F32), shape((864, 864), F32), shape((32, 32), F32),
            shape((64, 64), F32), shape((32, 108), F32), shape((64, 864), F32),
        ),
        in_specs=[VM] * 3,
        out_specs=(pl.BlockSpec(memory_space=pl.ANY),) * 7,
        scratch_shapes=[
            buf((64, 1, 16, 64), BF16), buf((108, 108), F32), buf((864, 864), F32), buf((32, 32), F32),
            buf((64, 64), F32), buf((32, 108), F32), buf((64, 864), F32), buf((512, 128), F32), dma((13,)),
        ],
        compiler_params=pltpu.CompilerParams(vmem_limit_bytes=VMEM_CAP),
    )(sums, late, feat)
    return features.transpose(0, 1, 3, 2), in_one, in_two, out_one, out_two, w_one.T, w_two.T


def solution(mesh):
    placed = (P(None, "batch", "space", None, None), P(), P(), P(None, "batch", "space", None))
    return jax.shard_map(
        local,
        mesh=mesh,
        in_specs=placed,
        out_specs=(P(None, "batch", None, "space"), P(), P(), P(), P(), P(), P()),
        check_vma=False,
    )
```

```python
import math

import jax
import jax.numpy as jnp
import numpy as np
from jax import lax
from jax.experimental import pallas as pl
from jax.experimental.pallas import tpu as pltpu
from jax.sharding import PartitionSpec as P

F32 = jnp.float32
BF16 = jnp.bfloat16
VMEM_CAP = 56 * 1024 * 1024
TOTAL_ONE = 2 * 128 * 64 * 64
TOTAL_TWO = 2 * 64 * 32 * 32


def tap_matrix():
    table = np.zeros((128, 3, 128), np.float32)
    for c in range(4):
        for a in range(3):
            for b in range(3):
                for e in range(3):
                    table[c * 27 + a * 9 + b * 3 + e, a, e * 20 + c * 5 + b] = 1
    return jnp.asarray(table.reshape(128, 384), F32)


def gelu_parts(value):
    square = value * value
    tangent = jnp.tanh(0.7978845608028654 * (value + 0.044715 * value * square))
    half = 0.5 * (1.0 + tangent)
    slope = half + 0.5 * value * (1.0 - tangent * tangent) * 0.7978845608028654 * (1.0 + 3.0 * 0.044715 * square)
    return value * half, slope


def dot(a, b):
    return lax.dot_general(a, b, (((1,), (0,)), ((), ())), preferred_element_type=F32)


def dot_nt(a, b):
    return lax.dot_general(a, b, (((1,), (1,)), ((), ())), preferred_element_type=F32)


def halves(value):
    high = value.astype(BF16)
    return high, (value - high.astype(F32)).astype(BF16)


VM = pl.BlockSpec(memory_space=pltpu.VMEM)
MESH = pl.DeviceIdType.MESH


def shifted(me, k):
    return (((me & 48) + (k & 48)) & 48) | (((me & 12) + (k & 12)) & 12) | (((me & 3) + (k & 3)) & 3)


def rows(index, count=16):
    return pl.ds(pl.multiple_of(index * count, count), count)


def await_bytes(ref, sem):
    pltpu.make_async_copy(ref, ref, sem).wait()


def spread_planes(first, count, load, vf, lf, of, uu, ee):
    def split(zz, carry):
        for c in range(4):
            at = zz * 4 + c
            vf[at, 8:136, :] = load(c, zz)
            for res in range(5):
                row = pl.ds(pl.multiple_of(at * 40 + res * 8, 8), 8)
                for m in range(4):
                    lf[row, m * 128 : (m + 1) * 128] = vf[at, pl.ds(7 + 4 * m + res, 8, stride=16), :]
        return carry

    lax.fori_loop(0, count, split, 0)
    parts = dot(lf[0 : count * 160, :].astype(BF16), ee[...])
    for zz in range(count):
        for res in range(5):
            of[zz * 1024 + res * 160 : zz * 1024 + (res + 1) * 160, :] = parts[
                zz * 160 : (zz + 1) * 160, res * 128 : (res + 1) * 128
            ]

    def flatten(zz, carry):
        for group in range(7):
            for j in range(8):
                start = zz * 1024 + group * 128 + j
                part = jnp.concatenate(
                    [of[pl.ds(start, 8, stride=8), :], of[pl.ds(start + 64, 8, stride=8), :]], axis=0
                )
                at = pl.ds(pl.multiple_of((first + zz) * 128 + group * 16, 16), 16)
                uu[at, j * 128 : (j + 1) * 128] = part.astype(BF16)
        uu[pl.ds(pl.multiple_of((first + zz) * 128 + 112, 16), 16), :] = jnp.zeros((16, 1024), BF16)
        return carry

    lax.fori_loop(0, count, flatten, 0)


def place_taps(act, a, p2f):
    lane = lax.broadcasted_iota(jnp.int32, (1, 1024), 1)
    for b in range(3):
        for e in range(3):
            p, q = (b + 1) % 2, (e + 1) % 2
            block = act[(p * 2 + q) * 32 : (p * 2 + q + 1) * 32, :]
            if e == 0:
                block = jnp.where(lane % 32 == 0, 0.0, pltpu.roll(block, 1, 1))
            if b == 0:
                block = jnp.where(lane < 32, 0.0, pltpu.roll(block, 32, 1))
            for j in range(8):
                p2f[j, pl.ds(a * 9 + b * 3 + e, 32, stride=27), :] = block[:, j * 128 : (j + 1) * 128]


def first_factor(uu, taps, tiles):
    gram = dot_nt(uu[0:384, :], uu[0:384, :]) + dot_nt(uu[256:640, :], uu[256:640, :])
    total = jnp.zeros((128, 128), F32)
    for part in halves(gram):
        for pq in range(4):
            tap = taps[:, pq * 384 : (pq + 1) * 384]
            total = total + dot(tap, dot_nt(part, tap).astype(BF16))
    total = total * (1.0 / TOTAL_ONE)
    for k in range(4):
        tiles[:, k * 128 : (k + 1) * 128] = total[k * 32 : (k + 1) * 32, :]


def group_matrix(pick):
    lane = lax.broadcasted_iota(jnp.int32, (128, 128), 0)
    col = lax.broadcasted_iota(jnp.int32, (128, 128), 1)
    for low in range(8):
        inside = (col >= low * 16) & (col < (low + 1) * 16)
        for x in range(4):
            hit = inside & (lane == x * 16 + col - low * 16)
            pick[low * 128 : (low + 1) * 128, x * 128 : (x + 1) * 128] = jnp.where(hit, 1.0, 0.0).astype(BF16)


def backward_weights(k2_ref, k2f, aa):
    k2f[:, 0:64] = k2_ref[...].astype(F32).T
    aa[...] = jnp.zeros((3, 128, 256), BF16)
    for a in range(3):
        for b in range(3):
            for e in range(3):
                p, q = (b + 1) % 2, (e + 1) % 2
                sy, sx = int(b == 0), int(e == 0)
                block = k2f[pl.ds(a * 9 + b * 3 + e, 32, stride=27), :]
                at = (p * 2 + q) * 32
                aa[a, at : at + 32, (sy * 2 + sx) * 64 : (sy * 2 + sx + 1) * 64] = block[:, 0:64].astype(BF16)


def layer_two_part(aa, a, plane):
    lane = lax.broadcasted_iota(jnp.int32, (1, 1024), 1)
    parts = lax.dot_general(aa[a], plane, (((0,), (0,)), ((), ())), preferred_element_type=F32)
    low = parts[0:64] + jnp.where(lane % 32 == 0, 0.0, pltpu.roll(parts[64:128], 1, 1))
    high = parts[128:192] + jnp.where(lane % 32 == 0, 0.0, pltpu.roll(parts[192:256], 1, 1))
    return low + jnp.where(lane < 32, 0.0, pltpu.roll(high, 32, 1))


def shift_back(value, gs, n):
    lane = lax.broadcasted_iota(jnp.int32, (1, 1024), 1)
    for sy in range(2):
        for sx in range(2):
            moved = value
            if sx:
                moved = jnp.where(lane % 32 == 31, 0.0, pltpu.roll(moved, 1023, 1))
            if sy:
                moved = jnp.where(lane >= 992, 0.0, pltpu.roll(moved, 992, 1))
            gs[n, (sy * 2 + sx) * 64 : (sy * 2 + sx + 1) * 64, :] = moved.astype(BF16)


def step_kernel(
    vol_hbm, k1_hbm, k2_hbm, cot_hbm, tap_hbm, out_hbm, late_hbm, feat_hbm,
    vol_ref, k1_ref, k2_ref, cot_ref, tap_ref, load_sem, vf, lf, of, uu, ee, taps, k1p, ww, slopes, hid, pre_two, p2f, p2b, tiles, sums, feat, feat_near, feat_mid, feat_far, pick, g2, k2f, aa, gs,
    rim, hid_in, g2_in, pair, half, got, piece, late, late_pair, late_x, late_sum, late_yz, late_total, late_far,
    rim_sem, hid_sem, g2_sem, pair_sem, late_pair_sem, rs_send, rs_recv, feat_sem, far_sem, x_sem, yz_sem,
    gather_send, gather_recv, back_sem, late_back_sem, keep_sem,
):
    me, core = lax.axis_index("space"), lax.axis_index("batch")
    sibling = (me, 1 - core)
    above, below = (lax.rem(me + 1, 64), core), (lax.rem(me + 63, 64), core)
    mine = pl.ds(pl.multiple_of(core * 256, 256), 256)
    other = pl.ds(pl.multiple_of((1 - core) * 256, 256), 256)

    def send(src, dst, sems, to):
        copy = pltpu.make_async_remote_copy(
            src_ref=src, dst_ref=dst, send_sem=sems.at[0], recv_sem=sems.at[1], device_id=to, device_id_type=MESH
        )
        copy.start()
        return copy

    barrier = pltpu.get_barrier_semaphore()
    pl.semaphore_signal(barrier, inc=1, device_id=sibling, device_id_type=MESH)

    for k in range(1, 64):
        pl.semaphore_signal(barrier, inc=1, device_id=(shifted(me, k), core), device_id_type=MESH)
    loads = [
        pltpu.make_async_copy(src, dst, load_sem.at[n])
        for n, (src, dst) in enumerate(
            ((vol_hbm, vol_ref), (tap_hbm, tap_ref), (k1_hbm, k1_ref), (k2_hbm, k2_ref), (cot_hbm, cot_ref))
        )
    ]
    for load in loads:
        load.start()

    at_x = lax.broadcasted_iota(jnp.int32, (128, 128), 0)
    lane = lax.broadcasted_iota(jnp.int32, (128, 128), 1)
    for m in range(4):
        for res in range(5):
            hit = (at_x == 4 * (lane - 32 * m) + (res - 1)) & (lane >= 32 * m) & (lane < 32 * (m + 1))
            ee[m * 128 : (m + 1) * 128, res * 128 : (res + 1) * 128] = jnp.where(hit, 1.0, 0.0).astype(BF16)
    vf[:, 0:8, :] = jnp.zeros((16, 8, 128), F32)
    for zz in range(4):
        of[zz * 1024 + 800 : zz * 1024 + 896, :] = jnp.zeros((96, 128), F32)
    for load in loads:
        load.wait()
    for pq, step in enumerate((0, 40, 2, 42)):
        moved = tap_ref[...] if step == 0 else pltpu.roll(tap_ref[...], step, 1)
        taps[:, pq * 384 : (pq + 1) * 384] = moved.astype(BF16)
    k1p[...] = jnp.zeros((32, 128), BF16)
    k1p[:, 0:108] = k1_ref[...]
    wide = dot(k1p[...], taps[...])
    for pq in range(4):
        ww[pq * 32 : (pq + 1) * 32, :] = wide[:, pq * 384 : (pq + 1) * 384].astype(BF16)

    pl.semaphore_wait(barrier, 64)
    rim_copy = send(vol_ref.at[:, 0, 3], rim, rim_sem, above)

    spread_planes(1, 4, lambda c, zz: vol_ref[c, 0, zz].astype(F32), vf, lf, of, uu, ee)
    act, slope = gelu_parts(dot(ww[...], uu[256:640, :]))
    slopes[128:256, :] = slope
    hid[...] = act.astype(BF16)
    hid_copy = send(hid, hid_in, hid_sem, above)
    place_taps(hid[...].astype(F32), 2, p2f)
    backward_weights(k2_ref, k2f, aa)
    pre_two[...] = layer_two_part(aa, 2, hid[...])

    group_matrix(pick)

    rim_copy.wait()
    spread_planes(
        0, 1, lambda c, zz: jnp.where(me > 0, rim[c].astype(F32), 0.0), vf, lf, of, uu, ee
    )
    act, slope = gelu_parts(dot(ww[...], uu[0:384, :]))
    slopes[0:128, :] = slope
    act = act.astype(BF16)
    place_taps(act.astype(F32), 1, p2f)
    pre_two[...] += layer_two_part(aa, 1, act)
    first_factor(uu, taps, tiles)

    hid_copy.wait()
    lower = jnp.where(me > 0, hid_in[...].astype(F32), 0.0)
    act, slope = gelu_parts(pre_two[...] + layer_two_part(aa, 0, lower.astype(BF16)))
    g2[...] = (cot_ref[...].astype(F32) * (1.0 / math.sqrt(TOTAL_TWO)) * slope).astype(BF16)
    g2_copy = send(g2, g2_in, g2_sem, below)

    act = act.astype(BF16).astype(F32)
    plane = me // 4
    left = lax.broadcasted_iota(jnp.int32, (1, 128), 1) < 64
    for tile in range(8):
        low, high = act[0:32, tile * 128 : (tile + 1) * 128], act[32:64, tile * 128 : (tile + 1) * 128]
        feat[2 * tile] = jnp.where(left, low, pltpu.roll(high, 64, 1)).astype(BF16)
        feat[2 * tile + 1] = jnp.where(left, pltpu.roll(low, 64, 1), high).astype(BF16)

    @pl.loop(1, 16)
    def _(k):
        to = shifted(me, 4 * k)
        send(feat.at[to // 4], feat_near.at[plane], feat_sem, (to, core))

    feat_near[plane] = feat[plane]

    place_taps(lower, 0, p2f)
    for j in range(8):
        p2b[0:864, j * 128 : (j + 1) * 128] = p2f[j].astype(BF16)
    p2b[864:896, :] = jnp.zeros((32, 1024), BF16)
    p2b[896:1280, :] = p2b[0:384, :]

    def gram_part(side):
        lanes = pl.ds(pl.multiple_of(side * 256, 256), 256)
        for i in range(7):
            cols = pl.ds(pl.multiple_of(i * 128 + side * 256, 128), 256)
            block = dot_nt(p2b[i * 128 : (i + 1) * 128, :], p2b[cols, :]) * (1.0 / TOTAL_TWO)
            sums[i * 128 : (i + 1) * 128, lanes] = block.astype(BF16)
        sums[864:896, lanes] = tiles[:, lanes].astype(BF16)

    def swap_rows(n, block):
        return send(sums.at[block, other], pair.at[block, :], pair_sem.at[n], sibling)

    def add_rows(block):
        half[block, :] = (sums[block, mine].astype(F32) + pair[block, :].astype(F32)).astype(BF16)

    def scatter(k, to):
        copy = pltpu.make_async_remote_copy(
            src_ref=half.at[rows(to), :], dst_ref=got.at[rows(k - 1), :], send_sem=rs_send,
            recv_sem=rs_recv.at[k // 16], device_id=(to, core), device_id_type=MESH,
        )
        copy.start()

    early, late_rows = slice(0, 896), slice(896, 1024)
    gram_part(1 - core)
    pair_copy = swap_rows(0, early)
    gram_part(core)
    pair_copy.wait()
    add_rows(early)

    @pl.loop(1, 64)
    def _(k):
        to = shifted(me, k)

        @pl.when(to < 56)
        def _():
            scatter(k, to)

    grads = dot_nt(g2[...], p2b[0:896, :])
    own = dot_nt(g2[...], g2[...])
    sums[896:960, :] = grads[:, 0:512].astype(BF16)
    sums[960:1024, 0:384] = grads[:, 512:896].astype(BF16)
    sums[960:1024, 384:512] = jnp.concatenate([own, jnp.zeros((64, 64), F32)], axis=1).astype(BF16)
    pair_copy = swap_rows(1, late_rows)
    shift_back(g2[...].astype(F32), gs, 0)
    pair_copy.wait()
    add_rows(late_rows)

    @pl.loop(1, 64)
    def _(k):
        to = shifted(me, k)

        @pl.when(to >= 56)
        def _():
            scatter(k, to)

    for sem in (feat_sem.at[0], feat_sem.at[1]):
        await_bytes(feat_near.at[0:15], sem)
    halves_wide = []
    for side in range(2):
        for k in range(16):
            block = feat_near[k].astype(F32)
            feat_mid[k * 32 : (k + 1) * 32, :] = pltpu.roll(block, 64, 1) if side else block
        halves_wide.append(
            jnp.concatenate([feat_mid[pl.ds(low, 64, stride=8), :] for low in range(8)], axis=1).astype(BF16)
        )
    wide = jnp.concatenate(halves_wide, axis=0)
    wide = dot(wide, pick[...]).astype(BF16)
    for x in range(4):
        feat_far[x] = wide[:, x * 128 : (x + 1) * 128]
    for k in range(1, 4):
        to = shifted(me, k)
        send(feat_far.at[to & 3], feat_hbm.at[me & 3], far_sem, (to, core))
    feat_keep = pltpu.make_async_copy(feat_far.at[me & 3], feat_hbm.at[me & 3], keep_sem.at[2])
    feat_keep.start()

    g2_copy.wait()
    shift_back(jnp.where(me < 63, g2_in[...].astype(F32), 0.0), gs, 1)
    cross = jnp.zeros((128, 384), F32)
    gram = jnp.zeros((128, 128), F32)
    for h in range(2):
        spread = dot(aa[h + 1], gs[0])
        if h == 1:
            spread = spread + dot(aa[0], gs[1])
        g1 = (spread * slopes[h * 128 : (h + 1) * 128, :]).astype(BF16)
        cross = cross + dot_nt(g1, uu[h * 256 : h * 256 + 384, :])
        gram = gram + dot_nt(g1, g1)
    weight = jnp.zeros((32, 128), F32)
    own = jnp.zeros((32, 32), F32)
    for pq in range(4):
        for part in halves(cross[pq * 32 : (pq + 1) * 32, :]):
            weight = weight + dot_nt(part, taps[:, pq * 384 : (pq + 1) * 384])
        own = own + gram[pq * 32 : (pq + 1) * 32, pq * 32 : (pq + 1) * 32]
    late[:, 0:128] = weight.astype(BF16)
    late[:, 128:256] = jnp.concatenate([own, jnp.zeros((32, 96), F32)], axis=1).astype(BF16)
    send(late.at[rows(1 - core), :], late_pair, late_pair_sem, sibling).wait()
    late_sum[...] = (late[rows(core), :].astype(F32) + late_pair[...].astype(F32)).astype(BF16)
    for k in range(1, 4):
        send(late_sum, late_x.at[k - 1], x_sem, (shifted(me, k), core))
    await_bytes(late_x, x_sem.at[0])
    await_bytes(late_x, x_sem.at[1])
    near = late_sum[...].astype(F32) + late_x[0].astype(F32) + (late_x[1].astype(F32) + late_x[2].astype(F32))
    late_total[...] = near.astype(BF16)
    for k in range(1, 16):
        send(late_total, late_yz.at[k - 1], yz_sem, (shifted(me, 4 * k), core))

    parts = [half[rows(me), :].astype(F32), jnp.zeros((16, 256), F32)]
    for group in range(4):
        slots = range(max(group * 16 - 1, 0), group * 16 + 15)
        await_bytes(got.at[slots[0] * 16 : slots[-1] * 16 + 16, :], rs_recv.at[group])
        for k in slots:
            parts[k % 2] = parts[k % 2] + got[k * 16 : (k + 1) * 16, :].astype(F32)
    piece[...] = (parts[0] + parts[1]).astype(BF16)
    place = out_hbm.at[rows(me), mine]
    keep = pltpu.make_async_copy(piece, place, keep_sem.at[0])
    keep.start()

    @pl.loop(1, 64)
    def _(k):
        copy = pltpu.make_async_remote_copy(
            src_ref=piece, dst_ref=place, send_sem=gather_send, recv_sem=gather_recv.at[k // 16],
            device_id=(shifted(me, k), core), device_id_type=MESH,
        )
        copy.start()

    backs = [feat_keep]
    keep.wait()
    for k in range(4):
        count = 240 if k == 0 else 256
        await_bytes(half.at[0:count, :], gather_recv.at[k])
        block = out_hbm.at[pl.ds(pl.multiple_of(lax.rem(me // 16 + 4 - k, 4) * 256, 256), 256), mine]
        backs.append(send(block, block, back_sem.at[k], sibling))
        if k == 0:
            await_bytes(late_yz, yz_sem.at[0])
            await_bytes(late_yz, yz_sem.at[1])
            far = late_total[...].astype(F32)
            for n in range(15):
                far = far + late_yz[n].astype(F32)
            late_far[...] = far
            place = late_hbm.at[rows(core), :]
            backs.append(pltpu.make_async_copy(late_far, place, keep_sem.at[1]))
            backs[-1].start()
            backs.append(send(late_far, place, late_back_sem, sibling))
    await_bytes(got, rs_send)
    await_bytes(got, gather_send)
    for sem in (far_sem.at[0], far_sem.at[1]):
        await_bytes(feat_far.at[0:3], sem)
    for copy in backs:
        copy.wait()


def unpack_kernel(
    sums_ref, late_ref, feat_ref,
    features_hbm, in_one_hbm, in_two_hbm, out_one_hbm, out_two_hbm, w_one_hbm, w_two_hbm,
    features_ref, in_one_ref, in_two, out_one_ref, out_two_ref, w_one_ref, w_two_ref, feat, store_sem,
):
    def store(src, dst):
        stores.append(pltpu.make_async_copy(src, dst, store_sem.at[len(stores)]))
        stores[-1].start()

    stores = []
    row = lax.broadcasted_iota(jnp.int32, (128, 128), 0)
    eye = jnp.where(row == lax.broadcasted_iota(jnp.int32, (128, 128), 1), 1.0, 0.0).astype(BF16)
    for i in range(7):
        height = min(128, 864 - i * 128)
        band = slice(i * 128, i * 128 + height)
        for k in range(-3, 4):
            j = (i + k) % 7
            width = min(128, 864 - j * 128)
            if k >= 0:
                block = sums_ref[i * 128 : (i + 1) * 128, k * 128 : (k + 1) * 128].astype(F32)
            else:
                block = dot_nt(eye, sums_ref[j * 128 : (j + 1) * 128, -k * 128 : (1 - k) * 128])
            in_two[band, j * 128 : j * 128 + width] = block[0:height, 0:width]
        store(in_two.at[band, :], in_two_hbm.at[band, :])
    w_two_ref[:, 0:512] = sums_ref[896:960, :].astype(F32)
    rest = sums_ref[960:1024, :].astype(F32)
    w_two_ref[:, 512:864] = rest[:, 0:352]
    out_two_ref[...] = rest[:, 384:448]
    first = sums_ref[864:896, :].astype(F32)
    for k in range(4):
        height = min(32, 108 - k * 32)
        in_one_ref[k * 32 : k * 32 + height, :] = first[0:height, k * 128 : k * 128 + 108]
    late = late_ref[...]
    w_one_ref[...] = late[:, 0:108]
    out_one_ref[...] = late[:, 128:160]
    for x in range(4):
        plane = feat_ref[x].astype(F32)
        for side in range(2):
            for yz in range(16):
                at, row = (yz * 4 + x) * 8 + side * 4, side * 64 + yz * 4
                feat[at : at + 4, :] = plane[row : row + 4, :]
    for r in range(8):
        block = feat[pl.ds(r, 64, stride=8), :]
        features_ref[r * 8 : (r + 1) * 8, 0, :, :] = dot_nt(eye, block.astype(BF16)).reshape(8, 16, 64).astype(BF16)
    store(w_two_ref, w_two_hbm)
    store(out_two_ref, out_two_hbm)
    store(in_one_ref, in_one_hbm)
    store(w_one_ref, w_one_hbm)
    store(out_one_ref, out_one_hbm)
    store(features_ref, features_hbm)
    for copy in stores:
        copy.wait()


def local(volume, kernel_one, kernel_two, cotangent):
    shape = jax.ShapeDtypeStruct
    dma = pltpu.SemaphoreType.DMA
    buf = pltpu.VMEM
    sums, late, feat = pl.pallas_call(
        step_kernel,
        name="step",
        out_shape=(shape((1024, 512), BF16), shape((32, 256), F32), shape((4, 128, 128), BF16)),
        in_specs=[pl.BlockSpec(memory_space=pl.ANY)] * 5,
        out_specs=(pl.BlockSpec(memory_space=pl.ANY),) * 3,
        scratch_shapes=[
            buf((4, 1, 4, 128, 128), BF16), buf((32, 108), BF16), buf((64, 864), BF16), buf((64, 1024), BF16),
            buf((128, 384), F32), dma((5,)),
            buf((16, 136, 128), F32), buf((640, 512), F32), buf((4096, 128), F32), buf((640, 1024), BF16),
            buf((512, 640), BF16), buf((128, 1536), BF16), buf((32, 128), BF16), buf((128, 384), BF16),
            buf((256, 1024), F32), buf((128, 1024), BF16), buf((64, 1024), F32), buf((8, 864, 128), F32), buf((1280, 1024), BF16),
            buf((32, 512), F32), buf((1024, 512), BF16), buf((16, 32, 128), BF16), buf((16, 32, 128), BF16), buf((512, 128), F32),
            buf((4, 128, 128), BF16), buf((1024, 512), BF16), buf((64, 1024), BF16),
            buf((864, 128), F32), buf((3, 128, 256), BF16), buf((2, 256, 1024), BF16),
            buf((4, 128, 128), BF16), buf((128, 1024), BF16), buf((64, 1024), BF16),
            buf((1024, 256), BF16), buf((1024, 256), BF16), buf((1008, 256), BF16), buf((16, 256), BF16),
            buf((32, 256), BF16), buf((16, 256), BF16), buf((3, 16, 256), BF16), buf((16, 256), BF16),
            buf((15, 16, 256), BF16), buf((16, 256), BF16), buf((16, 256), F32),
            dma((2,)), dma((2,)), dma((2,)), dma((2, 2)), dma((2,)), dma, dma((4,)), dma((2,)), dma((2,)), dma((2,)),
            dma((2,)), dma, dma((4,)), dma((4, 2)), dma((2,)), dma((3,)),
        ],
        compiler_params=pltpu.CompilerParams(
            vmem_limit_bytes=VMEM_CAP, collective_id=0, has_side_effects=True
        ),
    )(volume, kernel_one.T, kernel_two.T, cotangent.reshape(64, 1024), tap_matrix())
    features, in_one, in_two, out_one, out_two, w_one, w_two = pl.pallas_call(
        unpack_kernel,
        name="unpack",
        out_shape=(
            shape((64, 1, 16, 64), BF16), shape((108, 108), F32), shape((864, 864), F32), shape((32, 32), F32),
            shape((64, 64), F32), shape((32, 108), F32), shape((64, 864), F32),
        ),
        in_specs=[VM] * 3,
        out_specs=(pl.BlockSpec(memory_space=pl.ANY),) * 7,
        scratch_shapes=[
            buf((64, 1, 16, 64), BF16), buf((108, 108), F32), buf((864, 864), F32), buf((32, 32), F32),
            buf((64, 64), F32), buf((32, 108), F32), buf((64, 864), F32), buf((512, 128), F32), dma((13,)),
        ],
        compiler_params=pltpu.CompilerParams(vmem_limit_bytes=VMEM_CAP),
    )(sums, late, feat)
    return features.transpose(0, 1, 3, 2), in_one, in_two, out_one, out_two, w_one.T, w_two.T


def solution(mesh):
    placed = (P(None, "batch", "space", None, None), P(), P(), P(None, "batch", "space", None))
    return jax.shard_map(
        local,
        mesh=mesh,
        in_specs=placed,
        out_specs=(P(None, "batch", None, "space"), P(), P(), P(), P(), P(), P()),
        check_vma=False,
    )
```

```python
import math

import jax
import jax.numpy as jnp
import numpy as np
from jax import lax
from jax.experimental import pallas as pl
from jax.experimental.pallas import tpu as pltpu
from jax.sharding import PartitionSpec as P

F32 = jnp.float32
BF16 = jnp.bfloat16
VMEM_CAP = 56 * 1024 * 1024
TOTAL_ONE = 2 * 128 * 64 * 64
TOTAL_TWO = 2 * 64 * 32 * 32


def tap_matrix():
    table = np.zeros((128, 3, 128), np.float32)
    for c in range(4):
        for a in range(3):
            for b in range(3):
                for e in range(3):
                    table[c * 27 + a * 9 + b * 3 + e, a, e * 20 + c * 5 + b] = 1
    return jnp.asarray(table.reshape(128, 384), F32)


def gelu_parts(value):
    square = value * value
    tangent = jnp.tanh(0.7978845608028654 * (value + 0.044715 * value * square))
    half = 0.5 * (1.0 + tangent)
    slope = half + 0.5 * value * (1.0 - tangent * tangent) * 0.7978845608028654 * (1.0 + 3.0 * 0.044715 * square)
    return value * half, slope


def dot(a, b):
    return lax.dot_general(a, b, (((1,), (0,)), ((), ())), preferred_element_type=F32)


def dot_nt(a, b):
    return lax.dot_general(a, b, (((1,), (1,)), ((), ())), preferred_element_type=F32)


def halves(value):
    high = value.astype(BF16)
    return high, (value - high.astype(F32)).astype(BF16)


VM = pl.BlockSpec(memory_space=pltpu.VMEM)
MESH = pl.DeviceIdType.MESH


def shifted(me, k):
    return (((me & 48) + (k & 48)) & 48) | (((me & 12) + (k & 12)) & 12) | (((me & 3) + (k & 3)) & 3)


def rows(index, count=16):
    return pl.ds(pl.multiple_of(index * count, count), count)


def await_bytes(ref, sem):
    pltpu.make_async_copy(ref, ref, sem).wait()


def spread_planes(first, count, load, vf, lf, of, uu, ee):
    def split(zz, carry):
        for c in range(4):
            at = zz * 4 + c
            vf[at, 8:136, :] = load(c, zz)
            for res in range(5):
                row = pl.ds(pl.multiple_of(at * 40 + res * 8, 8), 8)
                for m in range(4):
                    lf[row, m * 128 : (m + 1) * 128] = vf[at, pl.ds(7 + 4 * m + res, 8, stride=16), :]
        return carry

    lax.fori_loop(0, count, split, 0)
    parts = dot(lf[0 : count * 160, :].astype(BF16), ee[...])
    for zz in range(count):
        for res in range(5):
            of[zz * 1024 + res * 160 : zz * 1024 + (res + 1) * 160, :] = parts[
                zz * 160 : (zz + 1) * 160, res * 128 : (res + 1) * 128
            ]

    def flatten(zz, carry):
        for group in range(7):
            for j in range(8):
                start = zz * 1024 + group * 128 + j
                part = jnp.concatenate(
                    [of[pl.ds(start, 8, stride=8), :], of[pl.ds(start + 64, 8, stride=8), :]], axis=0
                )
                at = pl.ds(pl.multiple_of((first + zz) * 128 + group * 16, 16), 16)
                uu[at, j * 128 : (j + 1) * 128] = part.astype(BF16)
        uu[pl.ds(pl.multiple_of((first + zz) * 128 + 112, 16), 16), :] = jnp.zeros((16, 1024), BF16)
        return carry

    lax.fori_loop(0, count, flatten, 0)


def place_taps(act, a, p2f):
    lane = lax.broadcasted_iota(jnp.int32, (1, 1024), 1)
    for b in range(3):
        for e in range(3):
            p, q = (b + 1) % 2, (e + 1) % 2
            block = act[(p * 2 + q) * 32 : (p * 2 + q + 1) * 32, :]
            if e == 0:
                block = jnp.where(lane % 32 == 0, 0.0, pltpu.roll(block, 1, 1))
            if b == 0:
                block = jnp.where(lane < 32, 0.0, pltpu.roll(block, 32, 1))
            for j in range(8):
                p2f[j, pl.ds(a * 9 + b * 3 + e, 32, stride=27), :] = block[:, j * 128 : (j + 1) * 128]


def first_factor(uu, taps, tiles):
    gram = dot_nt(uu[0:384, :], uu[0:384, :]) + dot_nt(uu[256:640, :], uu[256:640, :])
    total = jnp.zeros((128, 128), F32)
    for part in halves(gram):
        for pq in range(4):
            tap = taps[:, pq * 384 : (pq + 1) * 384]
            total = total + dot(tap, dot_nt(part, tap).astype(BF16))
    total = total * (1.0 / TOTAL_ONE)
    for k in range(4):
        tiles[:, k * 128 : (k + 1) * 128] = total[k * 32 : (k + 1) * 32, :]


def group_matrix(pick):
    lane = lax.broadcasted_iota(jnp.int32, (128, 128), 0)
    col = lax.broadcasted_iota(jnp.int32, (128, 128), 1)
    for low in range(8):
        inside = (col >= low * 16) & (col < (low + 1) * 16)
        for x in range(4):
            hit = inside & (lane == x * 16 + col - low * 16)
            pick[low * 128 : (low + 1) * 128, x * 128 : (x + 1) * 128] = jnp.where(hit, 1.0, 0.0).astype(BF16)


def backward_weights(k2_ref, k2f, aa):
    k2f[:, 0:64] = k2_ref[...].astype(F32).T
    aa[...] = jnp.zeros((3, 128, 256), BF16)
    for a in range(3):
        for b in range(3):
            for e in range(3):
                p, q = (b + 1) % 2, (e + 1) % 2
                sy, sx = int(b == 0), int(e == 0)
                block = k2f[pl.ds(a * 9 + b * 3 + e, 32, stride=27), :]
                at = (p * 2 + q) * 32
                aa[a, at : at + 32, (sy * 2 + sx) * 64 : (sy * 2 + sx + 1) * 64] = block[:, 0:64].astype(BF16)


def layer_two_part(aa, a, plane):
    lane = lax.broadcasted_iota(jnp.int32, (1, 1024), 1)
    parts = lax.dot_general(aa[a], plane, (((0,), (0,)), ((), ())), preferred_element_type=F32)
    low = parts[0:64] + jnp.where(lane % 32 == 0, 0.0, pltpu.roll(parts[64:128], 1, 1))
    high = parts[128:192] + jnp.where(lane % 32 == 0, 0.0, pltpu.roll(parts[192:256], 1, 1))
    return low + jnp.where(lane < 32, 0.0, pltpu.roll(high, 32, 1))


def shift_back(value, gs, n):
    lane = lax.broadcasted_iota(jnp.int32, (1, 1024), 1)
    for sy in range(2):
        for sx in range(2):
            moved = value
            if sx:
                moved = jnp.where(lane % 32 == 31, 0.0, pltpu.roll(moved, 1023, 1))
            if sy:
                moved = jnp.where(lane >= 992, 0.0, pltpu.roll(moved, 992, 1))
            gs[n, (sy * 2 + sx) * 64 : (sy * 2 + sx + 1) * 64, :] = moved.astype(BF16)


def step_kernel(
    vol_hbm, k1_hbm, k2_hbm, cot_hbm, tap_hbm, out_hbm, late_hbm, feat_hbm,
    vol_ref, k1_ref, k2_ref, cot_ref, tap_ref, load_sem, vf, lf, of, uu, ee, taps, k1p, ww, slopes, hid, pre_two, p2f, p2b, tiles, sums, feat, feat_near, feat_mid, feat_far, pick, g2, k2f, aa, gs,
    rim, hid_in, g2_in, pair, half, got, piece, late, late_pair, late_x, late_sum, late_yz, late_total, late_far,
    rim_sem, hid_sem, g2_sem, pair_sem, late_pair_sem, rs_send, rs_recv, feat_sem, far_sem, x_sem, yz_sem,
    gather_send, gather_recv, back_sem, late_back_sem, keep_sem,
):
    me, core = lax.axis_index("space"), lax.axis_index("batch")
    sibling = (me, 1 - core)
    above, below = (lax.rem(me + 1, 64), core), (lax.rem(me + 63, 64), core)
    mine = pl.ds(pl.multiple_of(core * 256, 256), 256)
    other = pl.ds(pl.multiple_of((1 - core) * 256, 256), 256)

    def send(src, dst, sems, to):
        copy = pltpu.make_async_remote_copy(
            src_ref=src, dst_ref=dst, send_sem=sems.at[0], recv_sem=sems.at[1], device_id=to, device_id_type=MESH
        )
        copy.start()
        return copy

    barrier = pltpu.get_barrier_semaphore()
    pl.semaphore_signal(barrier, inc=1, device_id=sibling, device_id_type=MESH)

    for k in range(1, 64):
        pl.semaphore_signal(barrier, inc=1, device_id=(shifted(me, k), core), device_id_type=MESH)
    loads = [
        pltpu.make_async_copy(src, dst, load_sem.at[n])
        for n, (src, dst) in enumerate(
            ((vol_hbm, vol_ref), (tap_hbm, tap_ref), (k1_hbm, k1_ref), (k2_hbm, k2_ref), (cot_hbm, cot_ref))
        )
    ]
    for load in loads:
        load.start()

    at_x = lax.broadcasted_iota(jnp.int32, (128, 128), 0)
    lane = lax.broadcasted_iota(jnp.int32, (128, 128), 1)
    for m in range(4):
        for res in range(5):
            hit = (at_x == 4 * (lane - 32 * m) + (res - 1)) & (lane >= 32 * m) & (lane < 32 * (m + 1))
            ee[m * 128 : (m + 1) * 128, res * 128 : (res + 1) * 128] = jnp.where(hit, 1.0, 0.0).astype(BF16)
    vf[:, 0:8, :] = jnp.zeros((16, 8, 128), F32)
    for zz in range(4):
        of[zz * 1024 + 800 : zz * 1024 + 896, :] = jnp.zeros((96, 128), F32)
    for load in loads:
        load.wait()
    for pq, step in enumerate((0, 40, 2, 42)):
        moved = tap_ref[...] if step == 0 else pltpu.roll(tap_ref[...], step, 1)
        taps[:, pq * 384 : (pq + 1) * 384] = moved.astype(BF16)
    k1p[...] = jnp.zeros((32, 128), BF16)
    k1p[:, 0:108] = k1_ref[...]
    wide = dot(k1p[...], taps[...])
    for pq in range(4):
        ww[pq * 32 : (pq + 1) * 32, :] = wide[:, pq * 384 : (pq + 1) * 384].astype(BF16)

    pl.semaphore_wait(barrier, 64)
    rim_copy = send(vol_ref.at[:, 0, 3], rim, rim_sem, above)

    spread_planes(1, 4, lambda c, zz: vol_ref[c, 0, zz].astype(F32), vf, lf, of, uu, ee)
    act, slope = gelu_parts(dot(ww[...], uu[256:640, :]))
    slopes[128:256, :] = slope
    hid[...] = act.astype(BF16)
    hid_copy = send(hid, hid_in, hid_sem, above)
    place_taps(hid[...].astype(F32), 2, p2f)
    backward_weights(k2_ref, k2f, aa)
    pre_two[...] = layer_two_part(aa, 2, hid[...])

    group_matrix(pick)

    rim_copy.wait()
    spread_planes(
        0, 1, lambda c, zz: jnp.where(me > 0, rim[c].astype(F32), 0.0), vf, lf, of, uu, ee
    )
    act, slope = gelu_parts(dot(ww[...], uu[0:384, :]))
    slopes[0:128, :] = slope
    act = act.astype(BF16)
    place_taps(act.astype(F32), 1, p2f)
    pre_two[...] += layer_two_part(aa, 1, act)
    first_factor(uu, taps, tiles)

    hid_copy.wait()
    lower = jnp.where(me > 0, hid_in[...].astype(F32), 0.0)
    act, slope = gelu_parts(pre_two[...] + layer_two_part(aa, 0, lower.astype(BF16)))
    g2[...] = (cot_ref[...].astype(F32) * (1.0 / math.sqrt(TOTAL_TWO)) * slope).astype(BF16)
    g2_copy = send(g2, g2_in, g2_sem, below)

    act = act.astype(BF16).astype(F32)
    plane = me // 4
    left = lax.broadcasted_iota(jnp.int32, (1, 128), 1) < 64
    for tile in range(8):
        low, high = act[0:32, tile * 128 : (tile + 1) * 128], act[32:64, tile * 128 : (tile + 1) * 128]
        feat[2 * tile] = jnp.where(left, low, pltpu.roll(high, 64, 1)).astype(BF16)
        feat[2 * tile + 1] = jnp.where(left, pltpu.roll(low, 64, 1), high).astype(BF16)

    @pl.loop(1, 16)
    def _(k):
        to = shifted(me, 4 * k)
        send(feat.at[to // 4], feat_near.at[plane], feat_sem, (to, core))

    feat_near[plane] = feat[plane]

    place_taps(lower, 0, p2f)
    for j in range(8):
        p2b[0:864, j * 128 : (j + 1) * 128] = p2f[j].astype(BF16)
    p2b[864:896, :] = jnp.zeros((32, 1024), BF16)
    p2b[896:1280, :] = p2b[0:384, :]

    def gram_part(side):
        lanes = pl.ds(pl.multiple_of(side * 256, 256), 256)
        for i in range(7):
            cols = pl.ds(pl.multiple_of(i * 128 + side * 256, 128), 256)
            block = dot_nt(p2b[i * 128 : (i + 1) * 128, :], p2b[cols, :]) * (1.0 / TOTAL_TWO)
            sums[i * 128 : (i + 1) * 128, lanes] = block.astype(BF16)
        sums[864:896, lanes] = tiles[:, lanes].astype(BF16)

    def swap_rows(n, block):
        return send(sums.at[block, other], pair.at[block, :], pair_sem.at[n], sibling)

    def add_rows(block):
        half[block, :] = (sums[block, mine].astype(F32) + pair[block, :].astype(F32)).astype(BF16)

    def scatter(k, to):
        copy = pltpu.make_async_remote_copy(
            src_ref=half.at[rows(to), :], dst_ref=got.at[rows(k - 1), :], send_sem=rs_send,
            recv_sem=rs_recv.at[k // 16], device_id=(to, core), device_id_type=MESH,
        )
        copy.start()

    early, late_rows = slice(0, 896), slice(896, 1024)
    gram_part(1 - core)
    pair_copy = swap_rows(0, early)
    gram_part(core)
    pair_copy.wait()
    add_rows(early)

    @pl.loop(1, 64)
    def _(k):
        to = shifted(me, k)

        @pl.when(to < 56)
        def _():
            scatter(k, to)

    grads = dot_nt(g2[...], p2b[0:896, :])
    own = dot_nt(g2[...], g2[...])
    sums[896:960, :] = grads[:, 0:512].astype(BF16)
    sums[960:1024, 0:384] = grads[:, 512:896].astype(BF16)
    sums[960:1024, 384:512] = jnp.concatenate([own, jnp.zeros((64, 64), F32)], axis=1).astype(BF16)
    pair_copy = swap_rows(1, late_rows)
    shift_back(g2[...].astype(F32), gs, 0)
    pair_copy.wait()
    add_rows(late_rows)

    @pl.loop(1, 64)
    def _(k):
        to = shifted(me, k)

        @pl.when(to >= 56)
        def _():
            scatter(k, to)

    for sem in (feat_sem.at[0], feat_sem.at[1]):
        await_bytes(feat_near.at[0:15], sem)
    halves_wide = []
    for side in range(2):
        for k in range(16):
            block = feat_near[k].astype(F32)
            feat_mid[k * 32 : (k + 1) * 32, :] = pltpu.roll(block, 64, 1) if side else block
        halves_wide.append(
            jnp.concatenate([feat_mid[pl.ds(low, 64, stride=8), :] for low in range(8)], axis=1).astype(BF16)
        )
    wide = jnp.concatenate(halves_wide, axis=0)
    wide = dot(wide, pick[...]).astype(BF16)
    for x in range(4):
        feat_far[x] = wide[:, x * 128 : (x + 1) * 128]
    for k in range(1, 4):
        to = shifted(me, k)
        send(feat_far.at[to & 3], feat_hbm.at[me & 3], far_sem, (to, core))
    feat_keep = pltpu.make_async_copy(feat_far.at[me & 3], feat_hbm.at[me & 3], keep_sem.at[2])
    feat_keep.start()

    g2_copy.wait()
    shift_back(jnp.where(me < 63, g2_in[...].astype(F32), 0.0), gs, 1)
    cross = jnp.zeros((128, 384), F32)
    gram = jnp.zeros((128, 128), F32)
    for h in range(2):
        spread = dot(aa[h + 1], gs[0])
        if h == 1:
            spread = spread + dot(aa[0], gs[1])
        g1 = (spread * slopes[h * 128 : (h + 1) * 128, :]).astype(BF16)
        cross = cross + dot_nt(g1, uu[h * 256 : h * 256 + 384, :])
        gram = gram + dot_nt(g1, g1)
    weight = jnp.zeros((32, 128), F32)
    own = jnp.zeros((32, 32), F32)
    for pq in range(4):
        for part in halves(cross[pq * 32 : (pq + 1) * 32, :]):
            weight = weight + dot_nt(part, taps[:, pq * 384 : (pq + 1) * 384])
        own = own + gram[pq * 32 : (pq + 1) * 32, pq * 32 : (pq + 1) * 32]
    late[:, 0:128] = weight.astype(BF16)
    late[:, 128:256] = jnp.concatenate([own, jnp.zeros((32, 96), F32)], axis=1).astype(BF16)
    send(late.at[rows(1 - core), :], late_pair, late_pair_sem, sibling).wait()
    late_sum[...] = (late[rows(core), :].astype(F32) + late_pair[...].astype(F32)).astype(BF16)
    for k in range(1, 4):
        send(late_sum, late_x.at[k - 1], x_sem, (shifted(me, k), core))
    await_bytes(late_x, x_sem.at[0])
    await_bytes(late_x, x_sem.at[1])
    near = late_sum[...].astype(F32) + late_x[0].astype(F32) + (late_x[1].astype(F32) + late_x[2].astype(F32))
    late_total[...] = near.astype(BF16)
    for k in range(1, 16):
        send(late_total, late_yz.at[k - 1], yz_sem, (shifted(me, 4 * k), core))

    parts = [half[rows(me), :].astype(F32), jnp.zeros((16, 256), F32)]
    for group in range(4):
        slots = range(max(group * 16 - 1, 0), group * 16 + 15)
        await_bytes(got.at[slots[0] * 16 : slots[-1] * 16 + 16, :], rs_recv.at[group])
        for k in slots:
            parts[k % 2] = parts[k % 2] + got[k * 16 : (k + 1) * 16, :].astype(F32)
    piece[...] = (parts[0] + parts[1]).astype(BF16)
    place = out_hbm.at[rows(me), mine]
    keep = pltpu.make_async_copy(piece, place, keep_sem.at[0])
    keep.start()

    @pl.loop(1, 64)
    def _(k):
        copy = pltpu.make_async_remote_copy(
            src_ref=piece, dst_ref=place, send_sem=gather_send, recv_sem=gather_recv.at[k // 4],
            device_id=(shifted(me, k), core), device_id_type=MESH,
        )
        copy.start()

    backs = [feat_keep]
    keep.wait()
    for k in range(16):
        count = 48 if k == 0 else 64
        await_bytes(half.at[0:count, :], gather_recv.at[k])
        line = shifted(me, ((4 - k // 4) % 4) * 16 + ((4 - k % 4) % 4) * 4) // 4
        block = out_hbm.at[rows(line, 64), mine]
        backs.append(send(block, block, back_sem.at[k], sibling))
        if k == 3:
            await_bytes(late_yz, yz_sem.at[0])
            await_bytes(late_yz, yz_sem.at[1])
            far = late_total[...].astype(F32)
            for n in range(15):
                far = far + late_yz[n].astype(F32)
            late_far[...] = far
            place = late_hbm.at[rows(core), :]
            backs.append(pltpu.make_async_copy(late_far, place, keep_sem.at[1]))
            backs[-1].start()
            backs.append(send(late_far, place, late_back_sem, sibling))
    await_bytes(got, rs_send)
    await_bytes(got, gather_send)
    for sem in (far_sem.at[0], far_sem.at[1]):
        await_bytes(feat_far.at[0:3], sem)
    for copy in backs:
        copy.wait()


def unpack_kernel(
    sums_ref, late_ref, feat_ref,
    features_hbm, in_one_hbm, in_two_hbm, out_one_hbm, out_two_hbm, w_one_hbm, w_two_hbm,
    features_ref, in_one_ref, in_two, out_one_ref, out_two_ref, w_one_ref, w_two_ref, feat, store_sem,
):
    def store(src, dst):
        stores.append(pltpu.make_async_copy(src, dst, store_sem.at[len(stores)]))
        stores[-1].start()

    stores = []
    row = lax.broadcasted_iota(jnp.int32, (128, 128), 0)
    eye = jnp.where(row == lax.broadcasted_iota(jnp.int32, (128, 128), 1), 1.0, 0.0).astype(BF16)
    for i in range(7):
        height = min(128, 864 - i * 128)
        band = slice(i * 128, i * 128 + height)
        for k in range(-3, 4):
            j = (i + k) % 7
            width = min(128, 864 - j * 128)
            if k >= 0:
                block = sums_ref[i * 128 : (i + 1) * 128, k * 128 : (k + 1) * 128].astype(F32)
            else:
                block = dot_nt(eye, sums_ref[j * 128 : (j + 1) * 128, -k * 128 : (1 - k) * 128])
            in_two[band, j * 128 : j * 128 + width] = block[0:height, 0:width]
        store(in_two.at[band, :], in_two_hbm.at[band, :])
    w_two_ref[:, 0:512] = sums_ref[896:960, :].astype(F32)
    rest = sums_ref[960:1024, :].astype(F32)
    w_two_ref[:, 512:864] = rest[:, 0:352]
    out_two_ref[...] = rest[:, 384:448]
    first = sums_ref[864:896, :].astype(F32)
    for k in range(4):
        height = min(32, 108 - k * 32)
        in_one_ref[k * 32 : k * 32 + height, :] = first[0:height, k * 128 : k * 128 + 108]
    late = late_ref[...]
    w_one_ref[...] = late[:, 0:108]
    out_one_ref[...] = late[:, 128:160]
    for x in range(4):
        plane = feat_ref[x].astype(F32)
        for side in range(2):
            for yz in range(16):
                at, row = (yz * 4 + x) * 8 + side * 4, side * 64 + yz * 4
                feat[at : at + 4, :] = plane[row : row + 4, :]
    for r in range(8):
        block = feat[pl.ds(r, 64, stride=8), :]
        features_ref[r * 8 : (r + 1) * 8, 0, :, :] = dot_nt(eye, block.astype(BF16)).reshape(8, 16, 64).astype(BF16)
    store(w_two_ref, w_two_hbm)
    store(out_two_ref, out_two_hbm)
    store(in_one_ref, in_one_hbm)
    store(w_one_ref, w_one_hbm)
    store(out_one_ref, out_one_hbm)
    store(features_ref, features_hbm)
    for copy in stores:
        copy.wait()


def local(volume, kernel_one, kernel_two, cotangent):
    shape = jax.ShapeDtypeStruct
    dma = pltpu.SemaphoreType.DMA
    buf = pltpu.VMEM
    sums, late, feat = pl.pallas_call(
        step_kernel,
        name="step",
        out_shape=(shape((1024, 512), BF16), shape((32, 256), F32), shape((4, 128, 128), BF16)),
        in_specs=[pl.BlockSpec(memory_space=pl.ANY)] * 5,
        out_specs=(pl.BlockSpec(memory_space=pl.ANY),) * 3,
        scratch_shapes=[
            buf((4, 1, 4, 128, 128), BF16), buf((32, 108), BF16), buf((64, 864), BF16), buf((64, 1024), BF16),
            buf((128, 384), F32), dma((5,)),
            buf((16, 136, 128), F32), buf((640, 512), F32), buf((4096, 128), F32), buf((640, 1024), BF16),
            buf((512, 640), BF16), buf((128, 1536), BF16), buf((32, 128), BF16), buf((128, 384), BF16),
            buf((256, 1024), F32), buf((128, 1024), BF16), buf((64, 1024), F32), buf((8, 864, 128), F32), buf((1280, 1024), BF16),
            buf((32, 512), F32), buf((1024, 512), BF16), buf((16, 32, 128), BF16), buf((16, 32, 128), BF16), buf((512, 128), F32),
            buf((4, 128, 128), BF16), buf((1024, 512), BF16), buf((64, 1024), BF16),
            buf((864, 128), F32), buf((3, 128, 256), BF16), buf((2, 256, 1024), BF16),
            buf((4, 128, 128), BF16), buf((128, 1024), BF16), buf((64, 1024), BF16),
            buf((1024, 256), BF16), buf((1024, 256), BF16), buf((1008, 256), BF16), buf((16, 256), BF16),
            buf((32, 256), BF16), buf((16, 256), BF16), buf((3, 16, 256), BF16), buf((16, 256), BF16),
            buf((15, 16, 256), BF16), buf((16, 256), BF16), buf((16, 256), F32),
            dma((2,)), dma((2,)), dma((2,)), dma((2, 2)), dma((2,)), dma, dma((4,)), dma((2,)), dma((2,)), dma((2,)),
            dma((2,)), dma, dma((16,)), dma((16, 2)), dma((2,)), dma((3,)),
        ],
        compiler_params=pltpu.CompilerParams(
            vmem_limit_bytes=VMEM_CAP, collective_id=0, has_side_effects=True
        ),
    )(volume, kernel_one.T, kernel_two.T, cotangent.reshape(64, 1024), tap_matrix())
    features, in_one, in_two, out_one, out_two, w_one, w_two = pl.pallas_call(
        unpack_kernel,
        name="unpack",
        out_shape=(
            shape((64, 1, 16, 64), BF16), shape((108, 108), F32), shape((864, 864), F32), shape((32, 32), F32),
            shape((64, 64), F32), shape((32, 108), F32), shape((64, 864), F32),
        ),
        in_specs=[VM] * 3,
        out_specs=(pl.BlockSpec(memory_space=pl.ANY),) * 7,
        scratch_shapes=[
            buf((64, 1, 16, 64), BF16), buf((108, 108), F32), buf((864, 864), F32), buf((32, 32), F32),
            buf((64, 64), F32), buf((32, 108), F32), buf((64, 864), F32), buf((512, 128), F32), dma((13,)),
        ],
        compiler_params=pltpu.CompilerParams(vmem_limit_bytes=VMEM_CAP),
    )(sums, late, feat)
    return features.transpose(0, 1, 3, 2), in_one, in_two, out_one, out_two, w_one.T, w_two.T


def solution(mesh):
    placed = (P(None, "batch", "space", None, None), P(), P(), P(None, "batch", "space", None))
    return jax.shard_map(
        local,
        mesh=mesh,
        in_specs=placed,
        out_specs=(P(None, "batch", None, "space"), P(), P(), P(), P(), P(), P()),
        check_vma=False,
    )
```
